256 devices in a mesh: px: 32 (over z, y), py: 8 (over x, core).
Axes of the slice: x: 4, y: 4, z: 8, core: 2. Of those that a mesh axis runs over, the one named last changes fastest.
Arguments:
- dofs: float32 [9, 20, 65536], P(None, None, ('px', 'py')), may hold values from -6 to 6
- star: float32 [3, 9, 9, 65536], P(None, None, None, ('px', 'py')), may hold values from -2 to 2
- flux_local: float32 [4, 9, 9, 65536], P(None, None, None, ('px', 'py')), may hold values from -0.5 to 0.5
- flux_neigh: float32 [4, 9, 9, 65536], P(None, None, None, ('px', 'py')), may hold values from -0.5 to 0.5
- time_stiff: float32 [3, 20, 20], replicated, may hold values from -1.25 to 1.25
- volume_stiff: float32 [3, 20, 20], replicated, may hold values from -0.15625 to 0.15625
- face_project: float32 [4, 10, 20], replicated, may hold values from -1.25 to 1.25
- face_rotate: float32 [3, 10, 10], replicated, may hold values from -2 to 2
- face_lift: float32 [4, 20, 10], replicated, may hold values from -2 to 2
- cluster: int32 [65536], P(('px', 'py')), may hold values from 0 to 1, as said below
- neighbors: int32 [4, 65536], P(None, ('px', 'py')), may hold values from -1 to 65535, as said below
- face_kind: int32 [4, 65536], P(None, ('px', 'py')), may hold values from 0 to 11
Outputs:
- solution: float32 [9, 20, 65536], P(None, None, ('px', 'py'))
The draws below stay inside these ranges and needn't reach their ends.
Inputs may be any that keep to these rules, and one draw needn't show every extreme that they name: 0 marks the fine cluster, 1 the coarse cluster. `neighbors`: devices are numbered px index times the devices along py plus py index, and element l of device r has global index r * 256 + l. -1 marks a face on the outer boundary. Every face has an element of the same device across it, except that an element with local index k * 32 + m (k < 4, m < 32) has at most one face whose neighbour lies on the device one step lower along px (k = 0), higher along px (k = 1), lower along py (k = 2) or higher along py (k = 3), at a local index from (k xor 1) * 32 to (k xor 1) * 32 + 31; where that device does not exist the face is -1.
All inputs are finite; a program needn't handle non-finite values.
Results may differ from the reference program's by a relative error of at most 0.0003.
Values sent between devices are 32-bit elements; how exact they have to be, the bound alone decides.
No kernel may reach another device: no remote copies, remote signals or barrier semaphores. Data moves between devices by JAX's collectives and lax.ppermute only.
A program may use at most 128 MiB of HBM per device.

```python
import math
from functools import partial
import jax
import jax.numpy as jnp
from jax import lax

QUANT = 9
BASIS = 20
FACE_BASIS = 10
ORDER = 4
SUBSTEPS = 4
E_DEV = 256
NS = 32
ELEMENTS = 65536
N_PX = 32
N_PY = 8


def draw_cluster(key, part):
    key = jax.random.fold_in(key, 11)
    first, second = jax.random.split(key)
    blocks = ELEMENTS // E_DEV
    share = jax.random.randint(first, (blocks, 1), E_DEV // 8, 7 * E_DEV // 8 + 1, dtype=jnp.int32)
    rolled = jax.random.randint(second, (blocks, E_DEV), 0, E_DEV, dtype=jnp.int32)
    return (rolled >= share).astype(jnp.int32).reshape(ELEMENTS)


def draw_neighbors(key, part):
    key = jax.random.fold_in(key, 23)
    first, second, third = jax.random.split(key, 3)
    index = jnp.arange(ELEMENTS, dtype=jnp.int32)
    device = index // E_DEV
    local = index % E_DEV
    row = device // N_PY
    column = device % N_PY
    inner = device[None, :] * E_DEV + jax.random.randint(first, (4, ELEMENTS), 0, E_DEV, dtype=jnp.int32)
    segment = local // NS
    target_row = row + jnp.where(segment == 0, -1, jnp.where(segment == 1, 1, 0))
    target_column = column + jnp.where(segment == 2, -1, jnp.where(segment == 3, 1, 0))
    inside = (target_row >= 0) & (target_row < N_PX) & (target_column >= 0) & (target_column < N_PY)
    opposite = jnp.bitwise_xor(segment, 1)
    position = jax.random.randint(second, (ELEMENTS,), 0, NS, dtype=jnp.int32)
    remote = jnp.where(inside, (target_row * N_PY + target_column) * E_DEV + opposite * NS + position, -1)
    which = jax.random.randint(third, (ELEMENTS,), 0, 4, dtype=jnp.int32)
    faces = jnp.arange(4, dtype=jnp.int32)[:, None]
    boundary = (local < 4 * NS)[None, :] & (faces == which[None, :])
    return jnp.where(boundary, remote[None, :], inner).astype(jnp.int32)


def with_ends(values, stream_key, low, top_value):
    longest = values.shape.index(max(values.shape))
    spots = []
    for shift in (0, 1):
        where = [jax.random.randint(jax.random.fold_in(stream_key, axis), (), 0, length) for axis, length in enumerate(values.shape)]
        where[longest] = (where[longest] + shift) % values.shape[longest]
        spots.append(tuple(where))
    return values.at[spots[0]].set(low).at[spots[1]].set(top_value)


def levels(own_key, dims, cuts, low, top_value):
    factor_of, own = 1.0, jax.random.fold_in(own_key, 6)
    for dim, blocks in cuts:
        heights = jnp.exp(jax.random.uniform(jax.random.fold_in(own, dim), (blocks,), jnp.float32, low / len(cuts), top_value / len(cuts)))
        factor_of = factor_of * jnp.repeat(heights, dims[dim] // blocks).reshape([-1 if axis == dim else 1 for axis in range(len(dims))])
    return factor_of


def noise(key, extent, width, bound, cuts=(), kind=jnp.bfloat16):
    drawn = width * jax.random.normal(key, extent, jnp.float32)
    if cuts:
        drawn = drawn * levels(key, extent, cuts, -0.22, 0.18)
    return jnp.clip(drawn, -bound, bound).astype(kind)


def setup_inputs(seed: int = 0) -> dict:
    keys = jax.random.split(jax.random.key(seed), 13)
    return {
        "dofs": noise(keys[0], (QUANT, BASIS, ELEMENTS), 1.0, 6.0, ((2, 256),), jnp.float32),
        "star": noise(keys[1], (3, QUANT, QUANT, ELEMENTS), QUANT ** -0.5, 2.0, ((3, 256),), jnp.float32),
        "flux_local": noise(keys[2], (4, QUANT, QUANT, ELEMENTS), (16 * QUANT) ** -0.5, 0.5, ((3, 256),), jnp.float32),
        "flux_neigh": noise(keys[3], (4, QUANT, QUANT, ELEMENTS), (16 * QUANT) ** -0.5, 0.5, ((3, 256),), jnp.float32),
        "time_stiff": noise(keys[4], (3, BASIS, BASIS), BASIS ** -0.5, 1.25, (), jnp.float32),
        "volume_stiff": noise(keys[5], (3, BASIS, BASIS), (64 * BASIS) ** -0.5, 0.15625, (), jnp.float32),
        "face_project": noise(keys[6], (4, FACE_BASIS, BASIS), BASIS ** -0.5, 1.25, (), jnp.float32),
        "face_rotate": noise(keys[7], (3, FACE_BASIS, FACE_BASIS), FACE_BASIS ** -0.5, 2.0, (), jnp.float32),
        "face_lift": noise(keys[8], (4, BASIS, FACE_BASIS), FACE_BASIS ** -0.5, 2.0, (), jnp.float32),
        "cluster": draw_cluster(jax.random.fold_in(keys[12], 71), 0),
        "neighbors": draw_neighbors(jax.random.fold_in(keys[12], 71), 0),
        "face_kind": with_ends(jax.random.randint(keys[11], (4, ELEMENTS), 0, 12), jax.random.fold_in(keys[11], 1), 0, 11).astype(jnp.int32),
    }


fine_step = 0.4
highest = lax.Precision.HIGHEST


def series(start, stop):
    return [(stop ** (power + 1) - start ** (power + 1)) / math.factorial(power + 1) for power in range(ORDER)]


def per_element(mats, field):
    return jnp.sum(mats[:, :, None, :] * field[None, :, :, :], axis=1)


def derivatives(time_stiff, dofs, star):
    terms = [dofs]
    for power in range(ORDER - 1):
        moved = jnp.einsum("dcb,qbe->dqce", time_stiff, terms[-1], precision=highest)
        total = per_element(star[0], moved[0]) + per_element(star[1], moved[1]) + per_element(star[2], moved[2])
        terms.append(-total)
    return jnp.stack(terms)


def integrate(derivs, coeffs):
    return jnp.sum(derivs * coeffs[:, None, None, :], axis=0)


def volume_term(own, star, volume_stiff):
    moved = jnp.einsum("dcb,qbe->dqce", volume_stiff, own, precision=highest)
    return per_element(star[0], moved[0]) + per_element(star[1], moved[1]) + per_element(star[2], moved[2])


def local_term(own, flux_local, face_project, face_lift):
    onface = jnp.einsum("ifb,qbe->iqfe", face_project, own, precision=highest)
    solved = jnp.stack([per_element(flux_local[face], onface[face]) for face in range(4)])
    return jnp.einsum("icf,iqfe->qce", face_lift, solved, precision=highest)


def neighbour_term(across, face_kind, flux_neigh, face_project, face_rotate, face_lift):
    sides = jnp.arange(4, dtype=jnp.int32)[:, None]
    turns = jnp.arange(3, dtype=jnp.int32)[:, None]
    solved = []
    for face in range(4):
        onface = jnp.einsum("jgb,qbe->jqge", face_project, across[face], precision=highest)
        pick_side = (face_kind[face][None, :] // 3 == sides).astype(jnp.float32)
        picked = jnp.sum(onface * pick_side[:, None, None, :], axis=0)
        rotated = jnp.einsum("hfg,qge->hqfe", face_rotate, picked, precision=highest)
        pick_turn = (face_kind[face][None, :] % 3 == turns).astype(jnp.float32)
        chosen = jnp.sum(rotated * pick_turn[:, None, None, :], axis=0)
        solved.append(per_element(flux_neigh[face], chosen))
    return jnp.einsum("icf,iqfe->qce", face_lift, jnp.stack(solved), precision=highest)


def update(volume_stiff, face_project, face_rotate, face_lift, dofs, star, flux_local, flux_neigh, own, across, face_kind, active):
    change = volume_term(own, star, volume_stiff) - local_term(own, flux_local, face_project, face_lift)
    change = change - neighbour_term(across, face_kind, flux_neigh, face_project, face_rotate, face_lift)
    return dofs + jnp.where(active[None, None, :], change, 0.0)


def blockwise(function, *arrays):
    blocks = ELEMENTS // E_DEV

    def split(array):
        return jnp.moveaxis(array.reshape(array.shape[:-1] + (blocks, E_DEV)), -2, 0)

    result = lax.map(lambda pieces: function(*pieces), tuple(split(array) for array in arrays))
    return jnp.moveaxis(result, 0, -2).reshape(result.shape[1:-1] + (ELEMENTS,))


def reference(dofs, star, flux_local, flux_neigh, time_stiff, volume_stiff, face_project, face_rotate, face_lift, cluster, neighbors, face_kind):
    fine = cluster == 0
    fine_coeffs = jnp.asarray(series(0.0, fine_step), dtype=jnp.float32)
    whole_coeffs = jnp.asarray(series(0.0, 2.0 * fine_step), dtype=jnp.float32)
    valid = neighbors >= 0
    target = jnp.where(valid, neighbors, 0)
    derivs = None
    earlier = None
    for step in range(SUBSTEPS):
        odd = step % 2 == 1
        fresh = blockwise(partial(derivatives, time_stiff), dofs, star)
        derivs = jnp.where(fine[None, None, None, :], fresh, derivs) if odd else fresh
        half = jnp.asarray(series((step % 2) * fine_step, (step % 2 + 1) * fine_step), dtype=jnp.float32)
        current = integrate(derivs, jnp.where(fine[None, :], fine_coeffs[:, None], half[:, None]))
        own = jnp.where(fine[None, None, :], current, integrate(derivs, whole_coeffs[:, None]))
        across = []
        for face in range(4):
            now = jnp.take(current, target[face], axis=2)
            if odd:
                now = jnp.where(fine[None, None, :], now, now + jnp.take(earlier, target[face], axis=2))
            across.append(jnp.where(valid[face][None, None, :], now, 0.0))
        across = jnp.stack(across)
        active = jnp.logical_or(fine, odd)
        dofs = blockwise(partial(update, volume_stiff, face_project, face_rotate, face_lift), dofs, star, flux_local, flux_neigh, own, across, face_kind, active)
        earlier = current
    return dofs
```

```python
import math
from functools import partial

import jax
import jax.numpy as jnp
from jax import lax
from jax.experimental import pallas as pl
from jax.experimental.pallas import tpu as pltpu
from jax.sharding import PartitionSpec as P

ORDER = 4
NS = 32
Q = 9
B = 24
FB = 16
LANES = 128
STATIC = 42
F32 = jnp.float32
BF16 = jnp.bfloat16
HIGHEST = lax.Precision.HIGHEST
STEP = 0.4


def series(start, stop):
    return [
        (stop ** (power + 1) - start ** (power + 1)) / math.factorial(power + 1)
        for power in range(ORDER)
    ]


FIRST = series(0.0, STEP)
SECOND = series(STEP, 2.0 * STEP)


def halves(x):
    high = x.astype(BF16)
    return high, (x - high.astype(F32)).astype(BF16)


def stacked(x):
    high = x.astype(BF16).astype(F32)
    rest = jnp.zeros((8, x.shape[1]), F32)
    return jnp.concatenate([high, x - high, high, rest], axis=0).astype(BF16)


def mm(a, b):
    return jnp.dot(a, b, preferred_element_type=F32)


def group(lg):
    return pl.ds(lg * LANES, LANES)


def transpose_quarters(four):
    quarter = lax.broadcasted_iota(jnp.int32, (8, LANES), 1) // NS
    out = []
    for k in range(4):
        total = None
        for m in range(4):
            shift = (NS * (m - k)) % LANES
            moved = pltpu.roll(four[m], shift, 1) if shift else four[m]
            total = moved if total is None else jnp.where(quarter == m, moved, total)
        out.append(total)
    return out


def spread(mat, width):
    rows = lax.broadcasted_iota(jnp.int32, (20, width), 0)
    cols = lax.broadcasted_iota(jnp.int32, (20, width), 1)
    both = ((cols == rows) | (cols == rows + B)).astype(F32)
    last = (cols == rows + 2 * B).astype(F32)
    high = mat.astype(BF16).astype(F32)
    low = (mat - high).astype(BF16).astype(F32)
    return mm(high.astype(BF16), both.astype(BF16)) + mm(low.astype(BF16), last.astype(BF16))


def prepare(time_ref, volume_ref, project_ref, rotate_ref, lift_ref, wt_ref, wb_ref, wl_ref, tmp_ref, big_ref):
    width = wt_ref.shape[1]
    tmp_ref[...] = jnp.zeros_like(tmp_ref)
    for d in range(3):
        tmp_ref[B * d : B * d + 20, :] = spread(-time_ref[d], width)
    wt_ref[...] = tmp_ref[: wt_ref.shape[0], :].astype(BF16)
    tmp_ref[...] = jnp.zeros_like(tmp_ref)
    for d in range(3):
        tmp_ref[B * d : B * d + 20, :] = spread(volume_ref[d], width)
    for j in range(4):
        at = 3 * B + FB * j
        tmp_ref[at : at + 10, :] = spread(project_ref[j], width)
    wb_ref[...] = tmp_ref[...].astype(BF16)
    rows = lax.broadcasted_iota(jnp.int32, (10, 256), 0)
    cols = lax.broadcasted_iota(jnp.int32, (10, 256), 1)
    total = jnp.zeros((20, 256), F32)
    for i in range(4):
        for t in range(3):
            part = jnp.dot(lift_ref[i], rotate_ref[t], precision=HIGHEST, preferred_element_type=F32)
            place = (cols == rows + (3 * i + t) * FB).astype(F32)
            total = total + jnp.dot(part, place, precision=HIGHEST, preferred_element_type=F32)
        place = (cols == rows + 192 + i * FB).astype(F32)
        total = total + jnp.dot(lift_ref[i], place, precision=HIGHEST, preferred_element_type=F32)
    high = total.astype(BF16).astype(F32)
    big_ref[...] = jnp.zeros_like(big_ref)
    big_ref[0:20, :] = high
    big_ref[32:52, :] = total - high
    wl_ref[...] = big_ref[...].astype(BF16)


def describe(nbr_ref, kind_ref, cluster_ref, star_ref, fluxn_ref, stat_ref):
    lanes = pl.ds(0, LANES)
    here = nbr_ref[0:1, LANES : 2 * LANES] >> 8
    remote = []
    for i in range(4):
        nbr = nbr_ref[i : i + 1, lanes]
        remote.append((nbr >= 0) & ((nbr >> 8) != here))
    spot = jnp.full((1, LANES), -1, jnp.int32)
    side = jnp.full((1, LANES), -1, jnp.int32)
    turn = jnp.full((1, LANES), -1, jnp.int32)
    face = jnp.full((1, LANES), -1, jnp.int32)
    for i in range(4):
        kind = kind_ref[i : i + 1, lanes]
        spot = jnp.where(remote[i], nbr_ref[i : i + 1, lanes] & (NS - 1), spot)
        side_i = (kind >= 3).astype(jnp.int32) + (kind >= 6).astype(jnp.int32) + (kind >= 9).astype(jnp.int32)
        side = jnp.where(remote[i], side_i, side)
        turn = jnp.where(remote[i], kind - 3 * side_i, turn)
        face = jnp.where(remote[i], i, face)
    weight = [jnp.where(r, 1.0, 0.0).astype(F32) for r in remote]
    stat_ref[27 + 3] = jnp.zeros((8, LANES), F32)
    for d in range(3):
        for p in range(Q):
            at = d * Q + p
            stat_ref[at] = star_ref[d, p, 0:8, lanes]
            stat_ref[27 + at // 8, at % 8 : at % 8 + 1] = star_ref[d, p, 8:9, lanes]
    stat_ref[41] = jnp.zeros((8, LANES), F32)
    for p in range(Q):
        total, last = None, None
        for i in range(4):
            term = fluxn_ref[i, p, 0:8, lanes] * weight[i]
            term_last = fluxn_ref[i, p, 8:9, lanes] * weight[i]
            total = term if total is None else total + term
            last = term_last if last is None else last + term_last
        stat_ref[31 + p] = total
        stat_ref[40 + p // 8, p % 8 : p % 8 + 1] = last
    fine = (cluster_ref[0:1, lanes] == 0).astype(F32)
    for row, value in enumerate((spot.astype(F32), side.astype(F32), turn.astype(F32), face.astype(F32), fine)):
        stat_ref[41, row + 1 : row + 2] = value


def stat_star(stat_ref):
    def at(d, p, q):
        n = d * Q + p
        return stat_ref[n, q : q + 1] if q < 8 else stat_ref[27 + n // 8, n % 8 : n % 8 + 1]

    return at


def stat_flux(stat_ref, p, q):
    return stat_ref[31 + p, q : q + 1] if q < 8 else stat_ref[40 + p // 8, p % 8 : p % 8 + 1]


def own_star(star_ref, lg):
    return lambda d, p, q: star_ref[d, p, q : q + 1, group(lg)]


def apply_star(star, moved_ref, lg):
    acc = [None] * Q
    for q in range(Q):
        for d in range(3):
            field = moved_ref[q, B * d : B * d + B, group(lg)]
            for p in range(Q):
                term = star(d, p, q) * field
                acc[p] = term if acc[p] is None else acc[p] + term
    return acc


def predict(dofs_ref, stars, wt_ref, term_ref, moved_ref, outs):
    width = LANES * len(stars)
    for power in range(ORDER - 1):
        source = term_ref if power else dofs_ref
        for q in range(Q):
            moved_ref[q, 0 : 3 * B, 0:width] = mm(wt_ref[...], stacked(source[q, :, 0:width]))[0 : 3 * B]
        for lg, star in enumerate(stars):
            acc = apply_star(star, moved_ref, lg)
            for p in range(Q):
                if power < ORDER - 2:
                    term_ref[p, :, group(lg)] = acc[p]
                for out_ref, coeffs in outs:
                    before = out_ref[p, :, group(lg)] if power else coeffs[0] * dofs_ref[p, :, group(lg)]
                    out_ref[p, :, group(lg)] = before + coeffs[power + 1] * acc[p]


def build_onehot(nbr_ref, kind_ref, hot_ref, tm_ref, groups):
    index = lax.broadcasted_iota(jnp.int32, (256, LANES), 0)
    here = nbr_ref[0:1, LANES : 2 * LANES] >> 8
    for lg in groups:
        for i in range(4):
            nbr = nbr_ref[i : i + 1, group(lg)]
            kind = kind_ref[i : i + 1, group(lg)]
            local = (nbr >= 0) & ((nbr >> 8) == here)
            side = (kind >= 3).astype(jnp.int32) + (kind >= 6).astype(jnp.int32) + (kind >= 9).astype(jnp.int32)
            turn = kind - 3 * side
            for j in range(4):
                pick = jnp.where(local & (side == j), nbr & 255, -1)
                hot = jnp.where(index == pick, 1.0, 0.0).astype(BF16)
                hot_ref[j * 256 : (j + 1) * 256, group(lg * 4 + i)] = hot
            for t in range(3):
                mask = jnp.where(turn == t, 1.0, 0.0).astype(F32)
                tm_ref[lg, i * 3 + t] = jnp.broadcast_to(mask, (FB, LANES)).astype(BF16)


def spread_and_project(cur_ref, wb_ref, moved_ref, face_ref, table_ref):
    for q in range(Q):
        got = mm(wb_ref[...], stacked(cur_ref[q, :, 0:256]))
        moved_ref[q, :, 0:256] = got[0 : 3 * B]
        for j in range(4):
            part = got[3 * B + FB * j : 3 * B + FB * (j + 1)]
            face_ref[j, q] = part
            high, low = halves(part)
            table_ref[q * FB : (q + 1) * FB, j * 256 : (j + 1) * 256] = high
            table_ref[(Q + q) * FB : (Q + q + 1) * FB, j * 256 : (j + 1) * 256] = low


def change_of(base_ref, cur_ref, out_ref, star_ref, fluxl_ref, fluxn_ref, wb_ref, wl_ref, s, groups):
    rows = Q * FB
    for lg in groups:
        for pair in range(2):
            cols = pl.ds((lg * 4 + 2 * pair) * LANES, 2 * LANES)
            got = mm(s["table"][...], s["hot"][:, cols])
            total = got[0:rows] + got[rows : 2 * rows]
            for half in range(2):
                s["across"][2 * pair + half] = total[:, half * LANES : (half + 1) * LANES]
        for i in range(4):
            for flux_ref, local in ((fluxl_ref, True), (fluxn_ref, False)):
                acc = [None] * Q
                for q in range(Q):
                    if local:
                        field = s["face"][i, q, :, group(lg)]
                    else:
                        field = s["across"][i, q * FB : (q + 1) * FB]
                    for p in range(Q):
                        term = flux_ref[i, p, q : q + 1, group(lg)] * field
                        acc[p] = term if acc[p] is None else acc[p] + term
                for p in range(Q):
                    high, low = halves(acc[p])
                    if local:
                        at = pl.ds(192 + i * FB, FB)
                        s["zh"][p, at, group(lg)] = high
                        s["zl"][p, at, group(lg)] = low
                    else:
                        for t in range(3):
                            at = pl.ds((3 * i + t) * FB, FB)
                            mask = s["tm"][lg, i * 3 + t]
                            s["zh"][p, at, group(lg)] = high * mask
                            s["zl"][p, at, group(lg)] = low * mask
        acc = apply_star(own_star(star_ref, lg), s["moved"], lg)
        for p in range(Q):
            out_ref[p, :, group(lg)] = base_ref[p, :, group(lg)] + acc[p]
    width = pl.ds(groups[0] * LANES, len(groups) * LANES)
    for p in range(Q):
        lifted = mm(wl_ref[...], s["zh"][p, :, width])
        rest = mm(wl_ref[0:32], s["zl"][p, :, width])
        out_ref[p, :, width] = out_ref[p, :, width] - (lifted[0:B] + lifted[32 : 32 + B] + rest[0:B])


def build_remote(stat_ref, rhot_ref, rm_ref):
    index = lax.broadcasted_iota(jnp.int32, (LANES, LANES), 0).astype(F32)
    spot, side, turn, face = (stat_ref[41, r : r + 1] for r in range(1, 5))
    segment = (lax.broadcasted_iota(jnp.int32, (1, LANES), 1) // NS * NS).astype(F32)
    spot = spot + segment
    for j in range(4):
        pick = jnp.where(side == float(j), spot, -1.0)
        rhot_ref[j * LANES : (j + 1) * LANES] = jnp.where(index == pick, 1.0, 0.0).astype(BF16)
    for i in range(4):
        for t in range(3):
            mask = jnp.where((face == float(i)) & (turn == float(t)), 1.0, 0.0).astype(F32)
            rm_ref[i * 3 + t] = jnp.broadcast_to(mask, (FB, LANES)).astype(BF16)


def project_remote(field_ref, lanes, wb_ref, table_ref):
    weights = wb_ref[3 * B - 8 :]
    for q in range(Q):
        got = mm(weights, stacked(field_ref[q, :, lanes]))
        for j in range(4):
            high, low = halves(got[8 + FB * j : 8 + FB * (j + 1)])
            table_ref[q * FB : (q + 1) * FB, j * LANES : (j + 1) * LANES] = high
            table_ref[(Q + q) * FB : (Q + q + 1) * FB, j * LANES : (j + 1) * LANES] = low


def remote_part(table_ref, stat_ref, rhot_ref, rm_ref, wl_ref, zh_ref, zl_ref):
    rows = Q * FB
    got = mm(table_ref[...], rhot_ref[...])
    across = got[0:rows] + got[rows : 2 * rows]
    acc = [None] * Q
    for q in range(Q):
        field = across[q * FB : (q + 1) * FB]
        for p in range(Q):
            term = stat_flux(stat_ref, p, q) * field
            acc[p] = term if acc[p] is None else acc[p] + term
    for p in range(Q):
        high, low = halves(acc[p])
        for c in range(12):
            zh_ref[p, c * FB : (c + 1) * FB] = high * rm_ref[c]
            zl_ref[p, c * FB : (c + 1) * FB] = low * rm_ref[c]
    out = []
    for p in range(Q):
        lifted = mm(wl_ref[:, 0:192], zh_ref[p])
        rest = mm(wl_ref[0:32, 0:192], zl_ref[p])
        out.append(lifted[0:B] + lifted[32 : 32 + B] + rest[0:B])
    return out


def pack(current_ref, other, stat_ref, msg_refs):
    blocks = []
    for p in range(Q):
        for r in range(3):
            blocks.append(current_ref[p, 8 * r : 8 * r + 8, 0:LANES])
    for p in range(Q):
        value = other(p)
        for r in range(3):
            blocks.append(value[8 * r : 8 * r + 8])
    if stat_ref is not None:
        blocks += [stat_ref[n] for n in range(STATIC)]
    while len(blocks) % 4:
        blocks.append(jnp.zeros((8, LANES), F32))
    for g in range(len(blocks) // 4):
        for k, value in enumerate(transpose_quarters(blocks[4 * g : 4 * g + 4])):
            msg_refs[k][g] = value


def unpack(msg_refs, first, last, store):
    for g in range(first // 4, -(-last // 4)):
        for m, value in enumerate(transpose_quarters([msg_refs[k][g] for k in range(4)])):
            if first <= 4 * g + m < last:
                store(4 * g + m - first, value)


def even_half(s, r, fine, dofs_ref, curo_ref, curb_ref, out_ref, msg_refs, stat_ref):
    stars = [own_star(r["star"], lg) for lg in range(2)]
    predict(dofs_ref, stars, r["wt"], s["term"], s["moved"], [(s["cur"], FIRST), (curo_ref, SECOND)])
    for p in range(Q):
        curb_ref[p] = s["cur"][p, :, 0:LANES]
    spread_and_project(s["cur"], r["wb"], s["moved"], s["face"], s["table"])
    change_of(dofs_ref, s["cur"], out_ref, r["star"], r["fluxl"], r["fluxn"], r["wb"], r["wl"], s, [0, 1])
    lead = fine[:, 0:LANES] > 0.5
    pack(
        s["cur"],
        lambda p: jnp.where(lead, out_ref[p, :, 0:LANES], curo_ref[p, :, 0:LANES]),
        stat_ref,
        msg_refs,
    )


def odd_half(s, r, fine, part_ref, curo_ref, curb_ref, recv_refs, stat_ref, ghost_ref, out_ref):
    def keep_table(n, value):
        s["gfield"][n // 3, 8 * (n % 3) : 8 * (n % 3) + 8, :] = value

    def keep_other(n, value):
        s["dofs"][n // 3, 8 * (n % 3) : 8 * (n % 3) + 8, 2 * LANES :] = value

    unpack(recv_refs, 0, 27, keep_table)
    unpack(recv_refs, 27, 54, keep_other)
    project_remote(s["gfield"], pl.ds(0, LANES), r["wb"], s["rtable"])
    project_remote(curb_ref, pl.ds(0, LANES), r["wb"], s["rtable2"])
    build_remote(stat_ref, s["rhot"], s["rm"])
    build_remote(ghost_ref, s["rhot2"], s["rm2"])
    mine = remote_part(s["rtable"], stat_ref, s["rhot"], s["rm"], r["wl"], s["rzh"], s["rzl"])
    for p in range(Q):
        s["dofs"][p, :, 0:LANES] = part_ref[p, :, 0:LANES] - mine[p]
        s["dofs"][p, :, LANES : 2 * LANES] = part_ref[p, :, LANES : 2 * LANES]
    theirs = remote_part(s["rtable2"], ghost_ref, s["rhot2"], s["rm2"], r["wl"], s["rzh"], s["rzl"])
    ghost_fine = ghost_ref[41, 5:6] > 0.5
    for p in range(Q):
        value = s["dofs"][p, :, 2 * LANES :]
        s["gfield"][p] = value
        s["dofs"][p, :, 2 * LANES :] = value - theirs[p]
    stars = [own_star(r["star"], 0), own_star(r["star"], 1), stat_star(ghost_ref)]
    predict(s["dofs"], stars, r["wt"], s["term"], s["moved"], [(s["cur"], FIRST)])
    for p in range(Q):
        s["cur"][p, :, 0:256] = jnp.where(fine > 0.5, s["cur"][p, :, 0:256], curo_ref[p])
        s["gfield"][p] = jnp.where(ghost_fine, s["cur"][p, :, 256:384], s["gfield"][p])
    project_remote(s["gfield"], pl.ds(0, LANES), r["wb"], s["rtable"])
    mine = remote_part(s["rtable"], stat_ref, s["rhot"], s["rm"], r["wl"], s["rzh"], s["rzl"])
    for p in range(Q):
        s["dofs"][p, :, 0:LANES] = s["dofs"][p, :, 0:LANES] - mine[p]
    spread_and_project(s["cur"], r["wb"], s["moved"], s["face"], s["table"])
    change_of(s["dofs"], s["cur"], out_ref, r["star"], r["fluxl"], r["fluxn"], r["wb"], r["wl"], s, [0, 1])


SCRATCH = {
    "dofs": ((Q, B, 384), F32),
    "cur": ((Q, B, 384), F32),
    "term": ((Q, B, 384), F32),
    "moved": ((Q, 3 * B, 384), F32),
    "face": ((4, Q, FB, 256), F32),
    "across": ((4, Q * FB, LANES), F32),
    "table": ((2 * Q * FB, 1024), BF16),
    "hot": ((1024, 1024), BF16),
    "tm": ((2, 12, FB, LANES), BF16),
    "zh": ((Q, 256, 256), BF16),
    "zl": ((Q, 256, 256), BF16),
}
REMOTE_SCRATCH = {
    "next": ((Q, B, 256), F32),
    "gfield": ((Q, B, LANES), F32),
    "rtable": ((2 * Q * FB, 512), BF16),
    "rtable2": ((2 * Q * FB, 512), BF16),
    "rhot": ((512, LANES), BF16),
    "rhot2": ((512, LANES), BF16),
    "rm": ((12, FB, LANES), BF16),
    "rm2": ((12, FB, LANES), BF16),
    "rzh": ((Q, 192, LANES), BF16),
    "rzl": ((Q, 192, LANES), BF16),
}


def call(kernel, name, ins, outs, scratch, inputs):
    def body(*refs):
        n, m = len(ins), len(outs)
        r = dict(zip(ins, refs[:n]))
        o = dict(zip(outs, refs[n : n + m]))
        s = dict(zip(scratch, refs[n + m :]))
        kernel(r, o, s)

    got = pl.pallas_call(
        body,
        out_shape=[jax.ShapeDtypeStruct(*outs[key]) for key in outs],
        scratch_shapes=[pltpu.VMEM(*scratch[key]) for key in scratch],
        compiler_params=pltpu.CompilerParams(vmem_limit_bytes=40 << 20),
        name=name,
    )(*(inputs[key] for key in ins))
    return dict(zip(outs, got))


def fine_of(cluster_ref):
    return (cluster_ref[...] == 0).astype(F32)


def first_kernel(r, o, s):
    prepare(
        r["time"], r["volume"], r["project"], r["rotate"], r["lift"],
        o["wt"], o["wb"], o["wl"], s["ptmp"], s["pbig"],
    )
    describe(r["nbr"], r["kind"], r["cluster"], r["star"], r["fluxn"], o["stat"])
    for p in range(Q):
        s["dofs"][p, 0:20, 0:256] = r["dofs"][p]
        s["dofs"][p, 20:B, 0:256] = jnp.zeros((B - 20, 256), F32)
    build_onehot(r["nbr"], r["kind"], s["hot"], s["tm"], [0, 1])
    r = dict(r, wt=o["wt"], wb=o["wb"], wl=o["wl"])
    msgs = [o["m%d" % k] for k in range(4)]
    even_half(s, r, fine_of(r["cluster"]), s["dofs"], o["curo"], o["curb"], o["part"], msgs, o["stat"])


def middle_kernel(r, o, s):
    build_onehot(r["nbr"], r["kind"], s["hot"], s["tm"], [0, 1])
    recv = [r["r%d" % k] for k in range(4)]

    def keep(n, value):
        o["ghost"][n] = value

    unpack(recv, 54, 54 + STATIC, keep)
    fine = fine_of(r["cluster"])
    odd_half(s, r, fine, r["part"], r["curo"], r["curb"], recv, r["stat"], o["ghost"], s["next"])
    msgs = [o["m%d" % k] for k in range(4)]
    even_half(s, r, fine, s["next"], o["curo"], o["curb"], o["part"], msgs, None)


def last_kernel(r, o, s):
    build_onehot(r["nbr"], r["kind"], s["hot"], s["tm"], [0, 1])
    recv = [r["r%d" % k] for k in range(4)]
    odd_half(s, r, fine_of(r["cluster"]), r["part"], r["curo"], r["curb"], recv, r["stat"], r["ghost"], s["next"])
    for p in range(Q):
        o["out"][p] = s["next"][p, 0:20, :]


def trade(got):
    lines = (("px", 1), ("px", -1), ("py", 1), ("py", -1))
    out = {}
    for k, (axis, step) in enumerate(lines):
        count = lax.axis_size(axis)
        if step > 0:
            pairs = [(i, i + 1) for i in range(count - 1)]
        else:
            pairs = [(i + 1, i) for i in range(count - 1)]
        out["r%d" % k] = lax.ppermute(got["m%d" % (k ^ 1)], axis, pairs)
    return out


def per_device(dofs, star, flux_local, flux_neigh, time_stiff, volume_stiff, face_project, face_rotate, face_lift, cluster, neighbors, face_kind):
    inputs = dict(
        dofs=dofs, star=star, fluxl=flux_local, fluxn=flux_neigh, time=time_stiff, volume=volume_stiff,
        project=face_project, rotate=face_rotate, lift=face_lift,
        cluster=cluster.reshape(1, 256), nbr=neighbors, kind=face_kind,
    )
    field = ((Q, B, 256), F32)
    state = {"part": field, "curo": field, "curb": ((Q, B, LANES), F32)}
    first = {
        **state,
        "wt": ((80, 80), BF16),
        "wb": ((144, 80), BF16),
        "wl": ((64, 256), BF16),
        "stat": ((STATIC, 8, LANES), F32),
        **{"m%d" % k: ((24, 8, LANES), F32) for k in range(4)},
    }
    got = call(
        first_kernel, "first", list(inputs), first,
        {**SCRATCH, "ptmp": ((144, 80), F32), "pbig": ((64, 256), F32)}, inputs,
    )
    inputs |= got
    inputs |= trade(got)
    shared = ["star", "fluxl", "fluxn", "wt", "wb", "wl", "cluster", "nbr", "kind", "stat", "part", "curo", "curb"]
    shared += ["r%d" % k for k in range(4)]
    middle = {
        **state,
        "ghost": ((STATIC, 8, LANES), F32),
        **{"m%d" % k: ((14, 8, LANES), F32) for k in range(4)},
    }
    got = call(middle_kernel, "middle", shared, middle, {**SCRATCH, **REMOTE_SCRATCH}, inputs)
    inputs |= got
    inputs |= trade(got)
    got = call(
        last_kernel, "last", shared + ["ghost"], {"out": ((Q, 20, 256), F32)},
        {**SCRATCH, **REMOTE_SCRATCH}, inputs,
    )
    return got["out"]


def solution(mesh):
    cells = ("px", "py")
    placed = (
        P(None, None, cells),
        P(None, None, None, cells),
        P(None, None, None, cells),
        P(None, None, None, cells),
        P(),
        P(),
        P(),
        P(),
        P(),
        P(cells),
        P(None, cells),
        P(None, cells),
    )
    return jax.shard_map(
        per_device,
        mesh=mesh,
        in_specs=placed,
        out_specs=P(None, None, cells),
        check_vma=False,
    )
```

```python
import math
from functools import partial

import jax
import jax.numpy as jnp
from jax import lax
from jax.experimental import pallas as pl
from jax.experimental.pallas import tpu as pltpu
from jax.sharding import PartitionSpec as P

ORDER = 4
NS = 32
Q = 9
B = 24
FB = 16
LANES = 128
KZ = 160
STATIC = 42
F32 = jnp.float32
BF16 = jnp.bfloat16
HIGHEST = lax.Precision.HIGHEST
STEP = 0.4
SENT = ("m0", "m1", "m2", "m3")
GOT = ("r0", "r1", "r2", "r3")


class Bag(dict):
    __getattr__ = dict.__getitem__
    __setattr__ = dict.__setitem__

    def __or__(self, other):
        return Bag({**self, **other})

    def pick(self, name, lg):
        return self[name + str(lg)]


def series(start, stop):
    return [
        (stop ** (power + 1) - start ** (power + 1)) / math.factorial(power + 1)
        for power in range(ORDER)
    ]


FIRST = series(0.0, STEP)
SECOND = series(STEP, 2.0 * STEP)


def halves(x):
    high = x.astype(BF16)
    return high, (x - high.astype(F32)).astype(BF16)


def stacked(x):
    high = x.astype(BF16).astype(F32)
    rest = jnp.zeros((8, x.shape[1]), F32)
    return jnp.concatenate([high, x - high, high, rest], axis=0).astype(BF16)


def mm(a, b):
    return jnp.dot(a, b, preferred_element_type=F32)


def group(lg):
    return pl.ds(lg * LANES, LANES)


def transpose_quarters(four):
    quarter = lax.broadcasted_iota(jnp.int32, (8, LANES), 1) // NS
    out = []
    for k in range(4):
        total = None
        for m in range(4):
            shift = (NS * (m - k)) % LANES
            moved = pltpu.roll(four[m], shift, 1) if shift else four[m]
            total = moved if total is None else jnp.where(quarter == m, moved, total)
        out.append(total)
    return out


def widened(block):
    high = block.astype(BF16).astype(F32)
    return (high + pltpu.roll(high, B, 1) + pltpu.roll(block - high, 2 * B, 1)).astype(BF16)


def prepare_predictor(time_ref, wt_ref, tmp_ref):
    tmp_ref[...] = jnp.zeros_like(tmp_ref)
    for d in range(3):
        tmp_ref[B * d : B * d + 20, 0:20] = -time_ref[d]
    wt_ref[...] = widened(tmp_ref[0:80])[:, 0:80]


def prepare(volume_ref, project_ref, rotate_ref, lift_ref, wb_ref, wl_ref, tmp_ref, turn_ref, big_ref):
    for d in range(3):
        tmp_ref[B * d : B * d + 20, 0:20] = volume_ref[d]
    for j in range(4):
        at = 3 * B + FB * j
        tmp_ref[at : at + 8, 0:20] = project_ref[0:8, j, :]
        for r in range(4):
            tmp_ref[at + 8 + r : at + 9 + r, 0:20] = project_ref[8:9, j, :]
            tmp_ref[at + 12 + r : at + 13 + r, 0:20] = project_ref[9:10, j, :]
    wb_ref[...] = widened(tmp_ref[...])[:, 0:80]
    turn_ref[...] = jnp.zeros_like(turn_ref)
    for t in range(3):
        turn_ref[0:10, FB * t : FB * t + 10] = rotate_ref[:, t, :]
    rows = lax.broadcasted_iota(jnp.int32, (10, 10), 0)
    cols = lax.broadcasted_iota(jnp.int32, (10, 10), 1)
    turn_ref[0:10, 3 * FB : 3 * FB + 10] = (rows == cols).astype(F32)
    turns = turn_ref[...].T[0:64, 0:16]
    big_ref[...] = jnp.zeros_like(big_ref)
    for i in range(4):
        big_ref[0:10, 32 * i : 32 * i + 20] = lift_ref[:, i, :]
    both = jnp.dot(turns, big_ref[0:16], precision=HIGHEST, preferred_element_type=F32)
    big_ref[0:16] = jnp.zeros((16, LANES), F32)
    for i in range(4):
        mine = pltpu.roll(both, LANES - 32 * i, 1) if i else both
        for t in range(4):
            at = (((i // 2) * 3 + t) if t < 3 else 6 + i // 2) * FB + 8 * (i % 2)
            big_ref[at : at + 8] = mine[FB * t : FB * t + 8]
            for g in (8, 9):
                at = 128 + 8 * t + 4 * (g - 8) + i
                big_ref[at : at + 1] = mine[FB * t + g : FB * t + g + 1]
    total = big_ref[...].T[0:32, 0:KZ]
    high = total.astype(BF16).astype(F32)
    wl_ref[...] = jnp.concatenate([high, total - high], axis=0).astype(BF16)


def describe(nbr_ref, kind_ref, cluster_ref, star_ref, fluxn_ref, stat_ref):
    lanes = pl.ds(0, LANES)
    here = nbr_ref[0:1, LANES : 2 * LANES] >> 8
    remote = []
    for i in range(4):
        nbr = nbr_ref[i : i + 1, lanes]
        remote.append((nbr >= 0) & ((nbr >> 8) != here))
    spot = jnp.full((1, LANES), -1, jnp.int32)
    side = jnp.full((1, LANES), -1, jnp.int32)
    turn = jnp.full((1, LANES), -1, jnp.int32)
    face = jnp.full((1, LANES), -1, jnp.int32)
    for i in range(4):
        kind = kind_ref[i : i + 1, lanes]
        spot = jnp.where(remote[i], nbr_ref[i : i + 1, lanes] & (NS - 1), spot)
        side_i = (kind >= 3).astype(jnp.int32) + (kind >= 6).astype(jnp.int32) + (kind >= 9).astype(jnp.int32)
        side = jnp.where(remote[i], side_i, side)
        turn = jnp.where(remote[i], kind - 3 * side_i, turn)
        face = jnp.where(remote[i], i, face)
    weight = [jnp.where(r, 1.0, 0.0).astype(F32) for r in remote]
    stat_ref[27 + 3] = jnp.zeros((8, LANES), F32)
    for d in range(3):
        for p in range(Q):
            at = d * Q + p
            stat_ref[at] = star_ref[p, 0:8, d, lanes]
            stat_ref[27 + at // 8, at % 8 : at % 8 + 1] = star_ref[p, 8, d : d + 1, lanes]
    stat_ref[41] = jnp.zeros((8, LANES), F32)
    for p in range(Q):
        total, last = None, None
        for i in range(4):
            term = fluxn_ref[p, 0:8, i, lanes] * weight[i]
            term_last = fluxn_ref[p, 8, i : i + 1, lanes] * weight[i]
            total = term if total is None else total + term
            last = term_last if last is None else last + term_last
        stat_ref[31 + p] = total
        stat_ref[40 + p // 8, p % 8 : p % 8 + 1] = last
    fine = (cluster_ref[0:1, lanes] == 0).astype(F32)
    for row, value in enumerate((spot.astype(F32), side.astype(F32), turn.astype(F32), face.astype(F32), fine)):
        stat_ref[41, row + 1 : row + 2] = value


def stat_star(stat_ref):
    def at(d, p, q):
        n = d * Q + p
        return stat_ref[n, q : q + 1] if q < 8 else stat_ref[27 + n // 8, n % 8 : n % 8 + 1]

    return at


def stat_flux(stat_ref, p, q):
    return stat_ref[31 + p, q : q + 1] if q < 8 else stat_ref[40 + p // 8, p % 8 : p % 8 + 1]


def own_star(star_ref, lg):
    return lambda d, p, q: star_ref[p, q, d : d + 1, group(lg)]


def apply_star(star, moved_ref, lanes):
    acc = [None] * Q
    for q in range(Q):
        for d in range(3):
            field = moved_ref[q, B * d : B * d + B, lanes]
            for p in range(Q):
                term = star(d, p, q) * field
                acc[p] = term if acc[p] is None else acc[p] + term
    return acc


def predict(dofs_ref, stars, wt_ref, term_ref, moved_ref, outs):
    width = LANES * len(stars)
    for power in range(ORDER - 1):
        source = term_ref if power else dofs_ref
        for q in range(Q):
            moved_ref[q, 0 : 3 * B, 0:width] = mm(wt_ref[...], stacked(source[q, :, 0:width]))[0 : 3 * B]
        for lg, star in enumerate(stars):
            acc = apply_star(star, moved_ref, group(lg))
            for p in range(Q):
                if power < ORDER - 2:
                    term_ref[p, :, group(lg)] = acc[p]
                for out_ref, coeffs in outs:
                    before = out_ref[p, :, group(lg)] if power else coeffs[0] * dofs_ref[p, :, group(lg)]
                    out_ref[p, :, group(lg)] = before + coeffs[power + 1] * acc[p]


def keep_masks(test, pair_ref, last_ref):
    for t in range(3):
        mask = [jnp.where(test(i, t), 1.0, 0.0).astype(F32) for i in range(4)]
        for pair in range(2):
            two = [jnp.broadcast_to(mask[2 * pair + n], (8, LANES)) for n in range(2)]
            pair_ref[pair * 3 + t] = jnp.concatenate(two, axis=0).astype(BF16)
        last_ref[t] = by_face(mask)


def by_face(four):
    which = lax.broadcasted_iota(jnp.int32, (8, LANES), 0) & 3
    total = jnp.broadcast_to(four[0], (8, LANES))
    for i in range(1, 4):
        total = jnp.where(which == i, four[i], total)
    return total


def keep_rows(flux_ref, lg, rows_ref):
    for p in range(Q):
        for q in range(Q):
            tile = flux_ref[p, q, :, group(lg)]
            rows_ref[p * Q + q, 0:4] = tile
            rows_ref[p * Q + q, 4:8] = tile


def fill_z(p, lanes, mains, last, pair_ref, last_ref, zh_ref, zl_ref):
    for pair in range(2):
        high, low = halves(jnp.concatenate(mains[2 * pair : 2 * pair + 2], axis=0))
        for t in range(3):
            at = pl.ds((pair * 3 + t) * FB, FB)
            zh_ref[p, at, lanes] = high * pair_ref[pair * 3 + t]
            zl_ref[p, at, lanes] = low * pair_ref[pair * 3 + t]
    return [last * last_ref[t] for t in range(3)]


def finish_z(p, lanes, turned, local, zh_ref, zl_ref):
    for n, two in enumerate(((turned[0], turned[1]), (turned[2], local))):
        high, low = halves(jnp.concatenate(two, axis=0))
        zh_ref[p, 128 + n * FB : 128 + (n + 1) * FB, lanes] = high
        zl_ref[p, 128 + n * FB : 128 + (n + 1) * FB, lanes] = low


def build_onehot(nbr_ref, kind_ref, s, groups):
    index = lax.broadcasted_iota(jnp.int32, (256, LANES), 0)
    here = nbr_ref[0:1, LANES : 2 * LANES] >> 8
    for lg in groups:
        turns = []
        for i in range(4):
            nbr = nbr_ref[i : i + 1, group(lg)]
            kind = kind_ref[i : i + 1, group(lg)]
            local = (nbr >= 0) & ((nbr >> 8) == here)
            side = (kind >= 3).astype(jnp.int32) + (kind >= 6).astype(jnp.int32) + (kind >= 9).astype(jnp.int32)
            turn = kind - 3 * side
            for j in range(4):
                pick = jnp.where(local & (side == j), nbr & 255, -1)
                hot = jnp.where(index == pick, 1.0, 0.0).astype(BF16)
                s.pick("hot", lg)[j * 256 : (j + 1) * 256, group(i)] = hot
            turns.append(turn)
        keep_masks(lambda i, t: turns[i] == t, s.pick("tm", lg), s.pick("um", lg))


def spread_and_project(cur_ref, wb_ref, s):
    for q in range(Q):
        got = mm(wb_ref[...], stacked(cur_ref[q, :, 0:256]))
        for lg in range(2):
            half = got[:, lg * LANES : (lg + 1) * LANES]
            s.pick("moved", lg)[q] = half[0 : 3 * B]
            for j in range(4):
                s.pick("face", lg)[j, q] = half[3 * B + FB * j : 3 * B + FB * (j + 1)]
        for j in range(4):
            high, low = halves(got[3 * B + FB * j : 3 * B + FB * (j + 1)])
            s.table[q * FB : (q + 1) * FB, j * 256 : (j + 1) * 256] = high
            s.table[(Q + q) * FB : (Q + q + 1) * FB, j * 256 : (j + 1) * 256] = low


def change_of(base, out, r, s, groups):
    rows = Q * FB
    for lg in groups:
        at_lg = group(groups.index(lg))
        for pair in range(2):
            cols = pl.ds(2 * pair * LANES, 2 * LANES)
            got = mm(s.table[...], s.pick("hot", lg)[:, cols])
            total = got[0:rows] + got[rows : 2 * rows]
            for half in range(2):
                s.across[2 * pair + half] = total[:, half * LANES : (half + 1) * LANES]
        face, across = s.pick("face", lg), s.across
        sources = (
            (r.fluxl, s.pick("fpl", lg), lambda i, q, rows: face[i, q, rows]),
            (r.fluxn, s.pick("fpn", lg), lambda i, q, rows: across[i, q * FB + rows.start : q * FB + rows.stop]),
        )
        got = []
        for flux_ref, rows_ref, field in sources:
            sums = []
            for i in range(5):
                acc = [None] * Q
                for q in range(Q):
                    if i < 4:
                        value = field(i, q, slice(0, 8))
                    else:
                        value = by_face([field(k, q, slice(8, 16)) for k in range(4)])
                    for p in range(Q):
                        scale = flux_ref[p, q, i : i + 1, group(lg)] if i < 4 else rows_ref[p * Q + q]
                        term = scale * value
                        acc[p] = term if acc[p] is None else acc[p] + term
                sums.append(acc)
            got.append(sums)
        local, other = got
        for p in range(Q):
            mains = [other[i][p] for i in range(4)]
            turned = fill_z(p, at_lg, mains, other[4][p], s.pick("tm", lg), s.pick("um", lg), s.zh, s.zl)
            for pair in range(2):
                high, low = halves(jnp.concatenate([local[2 * pair][p], local[2 * pair + 1][p]], axis=0))
                s.zh[p, 96 + pair * FB : 96 + (pair + 1) * FB, at_lg] = high
                s.zl[p, 96 + pair * FB : 96 + (pair + 1) * FB, at_lg] = low
            finish_z(p, at_lg, turned, local[4][p], s.zh, s.zl)
        acc = apply_star(own_star(r.star, lg), s.pick("moved", lg), group(0))
        for p in range(Q):
            out[lg][p] = base[lg][p] + acc[p]
    width = len(groups) * LANES
    for p in range(Q):
        lifted = mm(r.wl[...], s.zh[p, :, 0:width])
        rest = mm(r.wl[0:32], s.zl[p, :, 0:width])
        total = lifted[0:B] + lifted[32 : 32 + B] + rest[0:B]
        for n, lg in enumerate(groups):
            out[lg][p] = out[lg][p] - total[:, n * LANES : (n + 1) * LANES]


def build_remote(stat_ref, rhot_ref, rm_ref, ru_ref):
    index = lax.broadcasted_iota(jnp.int32, (LANES, LANES), 0).astype(F32)
    spot, side, turn, face = (stat_ref[41, r : r + 1] for r in range(1, 5))
    segment = (lax.broadcasted_iota(jnp.int32, (1, LANES), 1) // NS * NS).astype(F32)
    spot = spot + segment
    for j in range(4):
        pick = jnp.where(side == float(j), spot, -1.0)
        rhot_ref[j * LANES : (j + 1) * LANES] = jnp.where(index == pick, 1.0, 0.0).astype(BF16)
    keep_masks(lambda i, t: (face == float(i)) & (turn == float(t)), rm_ref, ru_ref)


def project_remote(field_ref, lanes, wb_ref, table_ref):
    weights = wb_ref[3 * B - 8 :]
    for q in range(Q):
        got = mm(weights, stacked(field_ref[q, :, lanes]))
        for j in range(4):
            high, low = halves(got[8 + FB * j : 8 + FB * (j + 1)])
            table_ref[q * FB : (q + 1) * FB, j * LANES : (j + 1) * LANES] = high
            table_ref[(Q + q) * FB : (Q + q + 1) * FB, j * LANES : (j + 1) * LANES] = low


def remote_part(table_ref, stat_ref, rhot_ref, rm_ref, ru_ref, wl_ref, zh_ref, zl_ref):
    rows = Q * FB
    got = mm(table_ref[...], rhot_ref[...])
    across = got[0:rows] + got[rows : 2 * rows]
    acc = [None] * Q
    for q in range(Q):
        field = across[q * FB : (q + 1) * FB]
        for p in range(Q):
            term = stat_flux(stat_ref, p, q) * field
            acc[p] = term if acc[p] is None else acc[p] + term
    nothing = jnp.zeros((8, LANES), F32)
    for p in range(Q):
        turned = fill_z(p, group(0), [acc[p][0:8]] * 4, acc[p][8:16], rm_ref, ru_ref, zh_ref, zl_ref)
        finish_z(p, group(0), turned, nothing, zh_ref, zl_ref)
    out = []
    for p in range(Q):
        lifted = mm(wl_ref[...], zh_ref[p])
        rest = mm(wl_ref[0:32], zl_ref[p])
        out.append(lifted[0:B] + lifted[32 : 32 + B] + rest[0:B])
    return out


def place_of(nbr_ref, columns):
    here = jnp.broadcast_to(nbr_ref[0:1, LANES : 2 * LANES] >> 8, (8, LANES))
    return (here // columns & 1) == 0, (here & 1) == 0


def pack(current_ref, other, stat_ref, msg_refs, even):
    blocks = []
    for p in range(Q):
        for r in range(3):
            blocks.append(current_ref[p, 8 * r : 8 * r + 8, 0:LANES])
    for p in range(Q):
        value = other(p)
        for r in range(3):
            blocks.append(value[8 * r : 8 * r + 8])
    if stat_ref is not None:
        blocks += [stat_ref[n] for n in range(STATIC)]
    while len(blocks) % 4:
        blocks.append(jnp.zeros((8, LANES), F32))
    for g in range(len(blocks) // 4):
        value = transpose_quarters(blocks[4 * g : 4 * g + 4])
        msg_refs[0][g] = jnp.where(even[0], value[1], value[0])
        msg_refs[1][g] = jnp.where(even[0], value[0], value[1])
        msg_refs[2][g] = jnp.where(even[1], value[2], value[3])
        msg_refs[3][g] = jnp.where(even[1], value[3], value[2])


def unpack(msg_refs, first, last, store, even):
    for g in range(first // 4, -(-last // 4)):
        one, two, three, last_one = (msg_refs[k][g] for k in range(4))
        four = [
            jnp.where(even[0], two, one),
            jnp.where(even[0], one, two),
            jnp.where(even[1], three, last_one),
            jnp.where(even[1], last_one, three),
        ]
        for m, value in enumerate(transpose_quarters(four)):
            if first <= 4 * g + m < last:
                store(4 * g + m - first, value)


def even_half(s, r, fine, dofs_ref, o, stat_ref):
    stars = [own_star(r.star, lg) for lg in range(2)]
    predict(dofs_ref, stars, r.wt, s.term, s.moved, [(s.cur, FIRST), (o.curo, SECOND)])
    for p in range(Q):
        o.curb[p] = s.cur[p, :, 0:LANES]
        o.base[p] = dofs_ref[p, :, LANES : 2 * LANES]
    spread_and_project(s.cur, r.wb, s)
    change_of([dofs_ref.at[:, :, 0:LANES]], [o.part0], r, s, [0])
    lead = fine[:, 0:LANES] > 0.5
    pack(
        s.cur,
        lambda p: jnp.where(lead, o.part0[p], o.curo[p, :, 0:LANES]),
        stat_ref,
        [o[key] for key in SENT],
        r.even,
    )


def rest_half(s, r, o):
    change_of([None, r.base], [None, o.part1], r, s, [1])
    project_remote(r.curb, pl.ds(0, LANES), r.wb, o.rtable2)


def odd_half(s, r, fine, ghost_ref, outs):
    def keep_table(n, value):
        s.gfield[n // 3, 8 * (n % 3) : 8 * (n % 3) + 8, :] = value

    def keep_other(n, value):
        s.dofs[n // 3, 8 * (n % 3) : 8 * (n % 3) + 8, 2 * LANES :] = value

    recv_refs = [r[key] for key in GOT]
    for p in range(Q):
        s.rzh[p, 96:128] = jnp.zeros((32, LANES), BF16)
        s.rzl[p, 96:128] = jnp.zeros((32, LANES), BF16)
    unpack(recv_refs, 0, 27, keep_table, r.even)
    unpack(recv_refs, 27, 54, keep_other, r.even)
    project_remote(s.gfield, pl.ds(0, LANES), r.wb, s.rtable)
    mine = remote_part(s.rtable, r.stat, r.rhot, r.rm, r.ru, r.wl, s.rzh, s.rzl)
    for p in range(Q):
        s.dofs[p, :, 0:LANES] = r.part0[p] - mine[p]
        s.dofs[p, :, LANES : 2 * LANES] = r.part1[p]
    theirs = remote_part(r.rtable2, ghost_ref, s.rhot2, s.rm2, s.ru2, r.wl, s.rzh, s.rzl)
    ghost_fine = ghost_ref[41, 5:6] > 0.5
    for p in range(Q):
        value = s.dofs[p, :, 2 * LANES :]
        s.gfield[p] = value
        s.dofs[p, :, 2 * LANES :] = value - theirs[p]
    stars = [own_star(r.star, 0), own_star(r.star, 1), stat_star(ghost_ref)]
    predict(s.dofs, stars, r.wt, s.term, s.moved, [(s.cur, FIRST)])
    for p in range(Q):
        s.cur[p, :, 0:256] = jnp.where(fine > 0.5, s.cur[p, :, 0:256], r.curo[p])
        s.gfield[p] = jnp.where(ghost_fine, s.cur[p, :, 256:384], s.gfield[p])
    project_remote(s.gfield, pl.ds(0, LANES), r.wb, s.rtable)
    mine = remote_part(s.rtable, r.stat, r.rhot, r.rm, r.ru, r.wl, s.rzh, s.rzl)
    for p in range(Q):
        s.dofs[p, :, 0:LANES] = s.dofs[p, :, 0:LANES] - mine[p]
    spread_and_project(s.cur, r.wb, s)
    halves_of = [s.dofs.at[:, :, group(lg)] for lg in range(2)]
    change_of(halves_of, outs, r, s, [0, 1])


FIELD = ((Q, B, LANES), F32)
SPREAD = dict(
    moved0=((Q, 3 * B, LANES), F32),
    face0=((4, Q, FB, LANES), F32),
)
KEPT = dict(
    moved1=((Q, 3 * B, LANES), F32),
    face1=((4, Q, FB, LANES), F32),
    table=((2 * Q * FB, 1024), BF16),
)
CHANGE = dict(
    across=((4, Q * FB, LANES), F32),
    zh=((Q, KZ, 256), BF16),
    zl=((Q, KZ, 256), BF16),
)
PREDICT = dict(
    dofs=((Q, B, 384), F32),
    cur=((Q, B, 384), F32),
    term=((Q, B, 384), F32),
    moved=((Q, 3 * B, 384), F32),
)
REMOTE = dict(
    gfield=FIELD,
    rtable=((2 * Q * FB, 512), BF16),
    rzh=((Q, KZ, LANES), BF16),
    rzl=((Q, KZ, LANES), BF16),
)
EVEN = dict(part0=FIELD, base=FIELD, curb=FIELD, curo=((Q, B, 256), F32), **KEPT)
GHOST_MASKS = dict(rhot2=((512, LANES), BF16), rm2=((6, FB, LANES), BF16), ru2=((3, 8, LANES), F32))
STAT = ((STATIC, 8, LANES), F32)
LOADED = ("star", "fluxl", "fluxn", "nbr", "kind", "cluster")
SMALL = ("time", "volume", "project", "rotate", "lift")


def masks(lg):
    shapes = dict(
        hot=((1024, 512), BF16), tm=((6, FB, LANES), BF16), um=((3, 8, LANES), F32),
        fpl=((Q * Q, 8, LANES), F32), fpn=((Q * Q, 8, LANES), F32),
    )
    return {key + str(lg): value for key, value in shapes.items()}


def messages(blocks):
    return {key: ((blocks // 4, 8, LANES), F32) for key in SENT}


def call(kernel, name, ins, outs, scratch, inputs, columns, hbm=False, flops=0):
    def body(*refs):
        n, m = len(ins), len(outs)
        r = Bag(zip(ins, refs[:n]))
        o = Bag(zip(outs, refs[n : n + m]))
        s = Bag(zip(scratch, refs[n + m : n + m + len(scratch)]))
        if hbm:
            sems = refs[-1]
            copies = {}
            for k, key in enumerate((*SMALL, "nbr", "kind", "cluster", "dofs", "star", "fluxn", "fluxl")):
                to = o[key] if key in LOADED else s[key + "_in"]
                copies[key] = pltpu.make_async_copy(r[key], to, sems.at[k])
                copies[key].start()
            r = Bag({key: o[key] if key in LOADED else s[key + "_in"] for key in ins})
            kernel(r, o, s, lambda *keys: [copies[key].wait() for key in keys], columns)
        else:
            r.even = place_of(r.nbr, columns)
            kernel(r, o, s)

    shapes = [pltpu.VMEM(*scratch[key]) for key in scratch]
    if hbm:
        shapes.append(pltpu.SemaphoreType.DMA((len(ins),)))
    space = pltpu.HBM if hbm else pltpu.VMEM
    got = pl.pallas_call(
        body,
        out_shape=[jax.ShapeDtypeStruct(*outs[key]) for key in outs],
        in_specs=[pl.BlockSpec(memory_space=space)] * len(ins),
        out_specs=[pl.BlockSpec(memory_space=pltpu.VMEM)] * len(outs),
        scratch_shapes=shapes,
        compiler_params=pltpu.CompilerParams(vmem_limit_bytes=24 << 20),
        cost_estimate=pl.CostEstimate(flops=flops, bytes_accessed=1 << 20, transcendentals=0),
        name=name,
    )(*(pltpu.with_memory_space_constraint(inputs[key], space) if hbm else inputs[key] for key in ins))
    return dict(zip(outs, got))


def fine_of(cluster_ref):
    return (cluster_ref[...] == 0).astype(F32)


def first_kernel(r, o, s, wait, columns):
    wait("time")
    prepare_predictor(r.time, o.wt, s.ptmp)
    wait("volume", "project", "rotate", "lift")
    prepare(r.volume, r.project, r.rotate, r.lift, o.wb, o.wl, s.ptmp, s.pturn, s.pbig)
    wait("nbr", "kind", "cluster")
    build_onehot(r.nbr, r.kind, o, [0])
    wait("dofs")
    for p in range(Q):
        s.dofs[p, 0:20, 0:256] = r.dofs[p]
        s.dofs[p, 20:B, 0:256] = jnp.zeros((B - 20, 256), F32)
    wait("star", "fluxn", "fluxl")
    keep_rows(r.fluxl, 0, o.fpl0)
    keep_rows(r.fluxn, 0, o.fpn0)
    describe(r.nbr, r.kind, r.cluster, r.star, r.fluxn, o.stat)
    r = Bag(r, wt=o.wt, wb=o.wb, wl=o.wl, even=place_of(r.nbr, columns))
    even_half(s | o, r, fine_of(r.cluster), s.dofs, o, o.stat)


def first_rest(r, o, s):
    build_onehot(r.nbr, r.kind, o, [1])
    keep_rows(r.fluxl, 1, o.fpl1)
    keep_rows(r.fluxn, 1, o.fpn1)
    build_remote(r.stat, o.rhot, o.rm, o.ru)
    rest_half(r | o | s, r, o)


def middle_kernel(r, o, s):
    def keep(n, value):
        o.ghost[n] = value

    unpack([r[key] for key in GOT], 54, 54 + STATIC, keep, r.even)
    build_remote(o.ghost, o.rhot2, o.rm2, o.ru2)
    fine = fine_of(r.cluster)
    s = r | s | o
    odd_half(s, r, fine, o.ghost, [s.next.at[:, :, group(lg)] for lg in range(2)])
    even_half(s, r, fine, s.next, o, None)


def second_rest(r, o, s):
    rest_half(r | o | s, r, o)


def last_kernel(r, o, s):
    s = r | s
    odd_half(s, r, fine_of(r.cluster), r.ghost, [s.next.at[:, :, group(lg)] for lg in range(2)])
    for p in range(Q):
        o.out[p] = s.next[p, 0:20, :]


def trade(got):
    out = {}
    for m, (axis, start) in enumerate((("px", 0), ("px", 1), ("py", 1), ("py", 0))):
        count = lax.axis_size(axis)
        pairs = []
        for low in range(start, count - 1, 2):
            pairs += [(low, low + 1), (low + 1, low)]
        out[GOT[m]] = lax.ppermute(got[SENT[m]], axis, pairs)
    return out


def per_device(dofs, star, flux_local, flux_neigh, time_stiff, volume_stiff, face_project, face_rotate, face_lift, cluster, neighbors, face_kind):
    columns = lax.axis_size("py")
    inputs = dict(
        dofs=dofs, star=star.transpose(1, 2, 0, 3), fluxl=flux_local.transpose(1, 2, 0, 3),
        fluxn=flux_neigh.transpose(1, 2, 0, 3), time=time_stiff, volume=volume_stiff,
        project=face_project.transpose(1, 0, 2), rotate=face_rotate.transpose(1, 0, 2), lift=face_lift.transpose(2, 0, 1),
        cluster=cluster.reshape(1, 256), nbr=neighbors, kind=face_kind,
    )
    first = {
        **{key: (inputs[key].shape, inputs[key].dtype) for key in LOADED},
        "wt": ((80, 80), BF16),
        "wb": ((144, 80), BF16),
        "wl": ((64, KZ), BF16),
        "stat": STAT,
        **masks(0),
        **EVEN,
        **messages(96),
    }
    scratch = {
        **PREDICT, **SPREAD, **CHANGE, "ptmp": ((144, LANES), F32), "pturn": ((LANES, LANES), F32), "pbig": ((256, LANES), F32),
        **{key + "_in": (inputs[key].shape, inputs[key].dtype) for key in (*SMALL, "dofs")},
    }
    weights = ["star", "fluxl", "fluxn", "wb", "wl", "nbr"]
    rest = {"part1": FIELD, "rtable2": ((2 * Q * FB, 512), BF16)}
    state = ["part0", "part1", "rtable2", "curo", *GOT]
    odd = weights + ["wt", "cluster", "stat", *masks(0), *masks(1), "rhot", "rm", "ru"] + state
    inputs |= call(first_kernel, "first", list(inputs), first, scratch, inputs, columns, hbm=True)
    inputs |= trade(inputs)
    inputs |= call(
        first_rest, "first_rest", weights + ["kind", "stat", "base", "curb", *KEPT],
        {**rest, **masks(1), "rhot": ((512, LANES), BF16), "rm": ((6, FB, LANES), BF16), "ru": ((3, 8, LANES), F32)},
        CHANGE, inputs, columns, flops=10**9,
    )
    both = {**PREDICT, **SPREAD, **CHANGE, **REMOTE, "next": ((Q, B, 256), F32)}
    inputs |= call(
        middle_kernel, "middle", odd, {"ghost": STAT, **GHOST_MASKS, **EVEN, **messages(56)}, both, inputs, columns,
    )
    inputs |= trade(inputs)
    inputs |= call(
        second_rest, "second_rest", weights + ["base", "curb", *masks(1), *KEPT], rest, CHANGE, inputs, columns,
        flops=10**9,
    )
    got = call(
        last_kernel, "last", odd + ["ghost", *GHOST_MASKS], {"out": ((Q, 20, 256), F32)}, {**both, **KEPT}, inputs, columns,
    )
    return got["out"]


def solution(mesh):
    cells = ("px", "py")
    placed = (
        P(None, None, cells),
        P(None, None, None, cells),
        P(None, None, None, cells),
        P(None, None, None, cells),
        P(),
        P(),
        P(),
        P(),
        P(),
        P(cells),
        P(None, cells),
        P(None, cells),
    )
    return jax.shard_map(
        per_device,
        mesh=mesh,
        in_specs=placed,
        out_specs=P(None, None, cells),
        check_vma=False,
    )
```

```python
import math
from functools import partial

import jax
import jax.numpy as jnp
from jax import lax
from jax.experimental import pallas as pl
from jax.experimental.pallas import tpu as pltpu
from jax.sharding import PartitionSpec as P

ORDER = 4
NS = 32
Q = 9
B = 24
FB = 16
LANES = 128
KZ = 160
STATIC = 42
F32 = jnp.float32
BF16 = jnp.bfloat16
HIGHEST = lax.Precision.HIGHEST
STEP = 0.4
SENT = ("m0", "m1", "m2", "m3")
GOT = ("r0", "r1", "r2", "r3")


class Bag(dict):
    __getattr__ = dict.__getitem__
    __setattr__ = dict.__setitem__

    def __or__(self, other):
        return Bag({**self, **other})

    def pick(self, name, lg):
        return self[name + str(lg)]


def series(start, stop):
    return [
        (stop ** (power + 1) - start ** (power + 1)) / math.factorial(power + 1)
        for power in range(ORDER)
    ]


FIRST = series(0.0, STEP)
SECOND = series(STEP, 2.0 * STEP)


def halves(x):
    high = x.astype(BF16)
    return high, (x - high.astype(F32)).astype(BF16)


def stacked(x):
    high = x.astype(BF16).astype(F32)
    rest = jnp.zeros((8, x.shape[1]), F32)
    return jnp.concatenate([high, x - high, high, rest], axis=0).astype(BF16)


def mm(a, b):
    return jnp.dot(a, b, preferred_element_type=F32)


def group(lg):
    return pl.ds(lg * LANES, LANES)


def transpose_quarters(four):
    quarter = lax.broadcasted_iota(jnp.int32, (8, LANES), 1) // NS
    out = []
    for k in range(4):
        total = None
        for m in range(4):
            shift = (NS * (m - k)) % LANES
            moved = pltpu.roll(four[m], shift, 1) if shift else four[m]
            total = moved if total is None else jnp.where(quarter == m, moved, total)
        out.append(total)
    return out


def widened(block):
    high = block.astype(BF16).astype(F32)
    return (high + pltpu.roll(high, B, 1) + pltpu.roll(block - high, 2 * B, 1)).astype(BF16)


def prepare_predictor(time_ref, wt_ref, tmp_ref):
    tmp_ref[...] = jnp.zeros_like(tmp_ref)
    for d in range(3):
        tmp_ref[B * d : B * d + 20, 0:20] = -time_ref[d]
    wt_ref[...] = widened(tmp_ref[0:80])[:, 0:80]


def prepare(volume_ref, project_ref, rotate_ref, lift_ref, wb_ref, wl_ref, tmp_ref, turn_ref, big_ref):
    for d in range(3):
        tmp_ref[B * d : B * d + 20, 0:20] = volume_ref[d]
    for j in range(4):
        at = 3 * B + FB * j
        tmp_ref[at : at + 8, 0:20] = project_ref[0:8, j, :]
        for r in range(4):
            tmp_ref[at + 8 + r : at + 9 + r, 0:20] = project_ref[8:9, j, :]
            tmp_ref[at + 12 + r : at + 13 + r, 0:20] = project_ref[9:10, j, :]
    wb_ref[...] = widened(tmp_ref[...])[:, 0:80]
    turn_ref[...] = jnp.zeros_like(turn_ref)
    for t in range(3):
        turn_ref[0:10, FB * t : FB * t + 10] = rotate_ref[:, t, :]
    rows = lax.broadcasted_iota(jnp.int32, (10, 10), 0)
    cols = lax.broadcasted_iota(jnp.int32, (10, 10), 1)
    turn_ref[0:10, 3 * FB : 3 * FB + 10] = (rows == cols).astype(F32)
    turns = turn_ref[...].T[0:64, 0:16]
    big_ref[...] = jnp.zeros_like(big_ref)
    for i in range(4):
        big_ref[0:10, 32 * i : 32 * i + 20] = lift_ref[:, i, :]
    both = jnp.dot(turns, big_ref[0:16], precision=HIGHEST, preferred_element_type=F32)
    big_ref[0:16] = jnp.zeros((16, LANES), F32)
    for i in range(4):
        mine = pltpu.roll(both, LANES - 32 * i, 1) if i else both
        for t in range(4):
            at = (((i // 2) * 3 + t) if t < 3 else 6 + i // 2) * FB + 8 * (i % 2)
            big_ref[at : at + 8] = mine[FB * t : FB * t + 8]
            for g in (8, 9):
                at = 128 + 8 * t + 4 * (g - 8) + i
                big_ref[at : at + 1] = mine[FB * t + g : FB * t + g + 1]
    total = big_ref[...].T[0:32, 0:KZ]
    high = total.astype(BF16).astype(F32)
    wl_ref[...] = jnp.concatenate([high, total - high], axis=0).astype(BF16)


def describe(nbr_ref, kind_ref, cluster_ref, star_ref, fluxn_ref, stat_ref):
    lanes = pl.ds(0, LANES)
    here = nbr_ref[0:1, LANES : 2 * LANES] >> 8
    remote = []
    for i in range(4):
        nbr = nbr_ref[i : i + 1, lanes]
        remote.append((nbr >= 0) & ((nbr >> 8) != here))
    spot = jnp.full((1, LANES), -1, jnp.int32)
    side = jnp.full((1, LANES), -1, jnp.int32)
    turn = jnp.full((1, LANES), -1, jnp.int32)
    face = jnp.full((1, LANES), -1, jnp.int32)
    for i in range(4):
        kind = kind_ref[i : i + 1, lanes]
        spot = jnp.where(remote[i], nbr_ref[i : i + 1, lanes] & (NS - 1), spot)
        side_i = (kind >= 3).astype(jnp.int32) + (kind >= 6).astype(jnp.int32) + (kind >= 9).astype(jnp.int32)
        side = jnp.where(remote[i], side_i, side)
        turn = jnp.where(remote[i], kind - 3 * side_i, turn)
        face = jnp.where(remote[i], i, face)
    weight = [jnp.where(r, 1.0, 0.0).astype(F32) for r in remote]
    stat_ref[27 + 3] = jnp.zeros((8, LANES), F32)
    for d in range(3):
        for p in range(Q):
            at = d * Q + p
            stat_ref[at] = star_ref[p, 0:8, d, lanes]
            stat_ref[27 + at // 8, at % 8 : at % 8 + 1] = star_ref[p, 8, d : d + 1, lanes]
    stat_ref[41] = jnp.zeros((8, LANES), F32)
    for p in range(Q):
        total, last = None, None
        for i in range(4):
            term = fluxn_ref[p, 0:8, i, lanes] * weight[i]
            term_last = fluxn_ref[p, 8, i : i + 1, lanes] * weight[i]
            total = term if total is None else total + term
            last = term_last if last is None else last + term_last
        stat_ref[31 + p] = total
        stat_ref[40 + p // 8, p % 8 : p % 8 + 1] = last
    fine = (cluster_ref[0:1, lanes] == 0).astype(F32)
    for row, value in enumerate((spot.astype(F32), side.astype(F32), turn.astype(F32), face.astype(F32), fine)):
        stat_ref[41, row + 1 : row + 2] = value


def stat_star(stat_ref):
    def at(d, p, q):
        n = d * Q + p
        return stat_ref[n, q : q + 1] if q < 8 else stat_ref[27 + n // 8, n % 8 : n % 8 + 1]

    return at


def stat_flux(stat_ref, p, q):
    return stat_ref[31 + p, q : q + 1] if q < 8 else stat_ref[40 + p // 8, p % 8 : p % 8 + 1]


def own_star(star_ref, lg):
    return lambda d, p, q: star_ref[p, q, d : d + 1, group(lg)]


def apply_star(star, moved_ref, lanes):
    acc = [None] * Q
    for q in range(Q):
        for d in range(3):
            field = moved_ref[q, B * d : B * d + B, lanes]
            for p in range(Q):
                term = star(d, p, q) * field
                acc[p] = term if acc[p] is None else acc[p] + term
    return acc


def predict(dofs_ref, stars, wt_ref, term_ref, moved_ref, outs):
    width = LANES * len(stars)
    for power in range(ORDER - 1):
        source = term_ref if power else dofs_ref
        for q in range(Q):
            moved_ref[q, 0 : 3 * B, 0:width] = mm(wt_ref[...], stacked(source[q, :, 0:width]))[0 : 3 * B]
        for lg, star in enumerate(stars):
            acc = apply_star(star, moved_ref, group(lg))
            for p in range(Q):
                if power < ORDER - 2:
                    term_ref[p, :, group(lg)] = acc[p]
                for out_ref, coeffs in outs:
                    before = out_ref[p, :, group(lg)] if power else coeffs[0] * dofs_ref[p, :, group(lg)]
                    out_ref[p, :, group(lg)] = before + coeffs[power + 1] * acc[p]


def keep_masks(test, pair_ref, last_ref):
    for t in range(3):
        mask = [jnp.where(test(i, t), 1.0, 0.0).astype(F32) for i in range(4)]
        for pair in range(2):
            two = [jnp.broadcast_to(mask[2 * pair + n], (8, LANES)) for n in range(2)]
            pair_ref[pair * 3 + t] = jnp.concatenate(two, axis=0).astype(BF16)
        last_ref[t] = by_face(mask)


def by_face(four):
    which = lax.broadcasted_iota(jnp.int32, (8, LANES), 0) & 3
    total = jnp.broadcast_to(four[0], (8, LANES))
    for i in range(1, 4):
        total = jnp.where(which == i, four[i], total)
    return total


def keep_rows(flux_ref, lg, rows_ref):
    for p in range(Q):
        for q in range(Q):
            tile = flux_ref[p, q, :, group(lg)]
            rows_ref[p * Q + q, 0:4] = tile
            rows_ref[p * Q + q, 4:8] = tile


def fill_z(lanes, mains, last, pair_ref, last_ref, zh_ref, zl_ref):
    for pair in range(2):
        high, low = halves(jnp.concatenate(mains[2 * pair : 2 * pair + 2], axis=0))
        for t in range(3):
            at = pl.ds((pair * 3 + t) * FB, FB)
            zh_ref[at, lanes] = high * pair_ref[pair * 3 + t]
            zl_ref[at, lanes] = low * pair_ref[pair * 3 + t]
    return [last * last_ref[t] for t in range(3)]


def finish_z(lanes, turned, local, zh_ref, zl_ref):
    for n, two in enumerate(((turned[0], turned[1]), (turned[2], local))):
        high, low = halves(jnp.concatenate(two, axis=0))
        zh_ref[128 + n * FB : 128 + (n + 1) * FB, lanes] = high
        zl_ref[128 + n * FB : 128 + (n + 1) * FB, lanes] = low


def lift(wl_ref, zh_ref, zl_ref, width, store):
    for start in range(0, Q * width, 2 * LANES):
        stop = min(start + 2 * LANES, Q * width)
        lifted = mm(wl_ref[...], zh_ref[:, start:stop])
        rest = mm(wl_ref[0:32], zl_ref[:, start:stop])
        total = lifted[0:B] + lifted[32 : 32 + B] + rest[0:B]
        for p in range(start // width, stop // width):
            store(p, total[:, p * width - start : (p + 1) * width - start])


def build_onehot(nbr_ref, kind_ref, s, groups):
    index = lax.broadcasted_iota(jnp.int32, (256, LANES), 0)
    here = nbr_ref[0:1, LANES : 2 * LANES] >> 8
    for lg in groups:
        turns = []
        for i in range(4):
            nbr = nbr_ref[i : i + 1, group(lg)]
            kind = kind_ref[i : i + 1, group(lg)]
            local = (nbr >= 0) & ((nbr >> 8) == here)
            side = (kind >= 3).astype(jnp.int32) + (kind >= 6).astype(jnp.int32) + (kind >= 9).astype(jnp.int32)
            turn = kind - 3 * side
            for j in range(4):
                pick = jnp.where(local & (side == j), nbr & 255, -1)
                hot = jnp.where(index == pick, 1.0, 0.0).astype(BF16)
                s.pick("hot", lg)[j * 256 : (j + 1) * 256, group(i)] = hot
            turns.append(turn)
        keep_masks(lambda i, t: turns[i] == t, s.pick("tm", lg), s.pick("um", lg))


def spread_and_project(cur_ref, wb_ref, s):
    for q in range(Q):
        got = mm(wb_ref[...], stacked(cur_ref[q, :, 0:256]))
        for lg in range(2):
            half = got[:, lg * LANES : (lg + 1) * LANES]
            s.pick("moved", lg)[q] = half[0 : 3 * B]
            for j in range(4):
                s.pick("face", lg)[j, q] = half[3 * B + FB * j : 3 * B + FB * (j + 1)]
        for j in range(4):
            high, low = halves(got[3 * B + FB * j : 3 * B + FB * (j + 1)])
            s.table[q * FB : (q + 1) * FB, j * 256 : (j + 1) * 256] = high
            s.table[(Q + q) * FB : (Q + q + 1) * FB, j * 256 : (j + 1) * 256] = low


def change_of(base, out, r, s, groups):
    rows = Q * FB
    for lg in groups:
        for pair in range(2):
            cols = pl.ds(2 * pair * LANES, 2 * LANES)
            got = mm(s.table[...], s.pick("hot", lg)[:, cols])
            total = got[0:rows] + got[rows : 2 * rows]
            for half in range(2):
                s.across[2 * pair + half] = total[:, half * LANES : (half + 1) * LANES]
        face, across = s.pick("face", lg), s.across
        sources = (
            (r.fluxl, s.pick("fpl", lg), lambda i, q, rows: face[i, q, rows]),
            (r.fluxn, s.pick("fpn", lg), lambda i, q, rows: across[i, q * FB + rows.start : q * FB + rows.stop]),
        )
        got = []
        for flux_ref, rows_ref, field in sources:
            sums = []
            for i in range(5):
                acc = [None] * Q
                for q in range(Q):
                    if i < 4:
                        value = field(i, q, slice(0, 8))
                    else:
                        value = by_face([field(k, q, slice(8, 16)) for k in range(4)])
                    for p in range(Q):
                        scale = flux_ref[p, q, i : i + 1, group(lg)] if i < 4 else rows_ref[p * Q + q]
                        term = scale * value
                        acc[p] = term if acc[p] is None else acc[p] + term
                sums.append(acc)
            got.append(sums)
        local, other = got
        for p in range(Q):
            mains = [other[i][p] for i in range(4)]
            at_lg = group(p * len(groups) + groups.index(lg))
            turned = fill_z(at_lg, mains, other[4][p], s.pick("tm", lg), s.pick("um", lg), s.zh, s.zl)
            for pair in range(2):
                high, low = halves(jnp.concatenate([local[2 * pair][p], local[2 * pair + 1][p]], axis=0))
                s.zh[96 + pair * FB : 96 + (pair + 1) * FB, at_lg] = high
                s.zl[96 + pair * FB : 96 + (pair + 1) * FB, at_lg] = low
            finish_z(at_lg, turned, local[4][p], s.zh, s.zl)
        acc = apply_star(own_star(r.star, lg), s.pick("moved", lg), group(0))
        for p in range(Q):
            out[lg][p] = base[lg][p] + acc[p]

    def store(p, total):
        for n, lg in enumerate(groups):
            out[lg][p] = out[lg][p] - total[:, n * LANES : (n + 1) * LANES]

    lift(r.wl, s.zh, s.zl, len(groups) * LANES, store)


def build_remote(stat_ref, rhot_ref, rm_ref, ru_ref):
    index = lax.broadcasted_iota(jnp.int32, (LANES, LANES), 0).astype(F32)
    spot, side, turn, face = (stat_ref[41, r : r + 1] for r in range(1, 5))
    segment = (lax.broadcasted_iota(jnp.int32, (1, LANES), 1) // NS * NS).astype(F32)
    spot = spot + segment
    for j in range(4):
        pick = jnp.where(side == float(j), spot, -1.0)
        rhot_ref[j * LANES : (j + 1) * LANES] = jnp.where(index == pick, 1.0, 0.0).astype(BF16)
    keep_masks(lambda i, t: (face == float(i)) & (turn == float(t)), rm_ref, ru_ref)


def project_remote(field_ref, wb_ref, table_ref):
    weights = wb_ref[3 * B - 8 :]
    fields = [stacked(field_ref[q]) for q in range(Q)]
    for start in range(0, Q, 2):
        two = fields[start : start + 2]
        got = mm(weights, jnp.concatenate(two, axis=1))
        for n in range(len(two)):
            q = start + n
            for j in range(4):
                high, low = halves(got[8 + FB * j : 8 + FB * (j + 1), n * LANES : (n + 1) * LANES])
                table_ref[q * FB : (q + 1) * FB, j * LANES : (j + 1) * LANES] = high
                table_ref[(Q + q) * FB : (Q + q + 1) * FB, j * LANES : (j + 1) * LANES] = low


def remote_z(table_ref, stat_ref, rhot_ref, rm_ref, ru_ref, s, place):
    rows = Q * FB
    got = mm(table_ref[...], rhot_ref[...])
    across = got[0:rows] + got[rows : 2 * rows]
    acc = [None] * Q
    for q in range(Q):
        field = across[q * FB : (q + 1) * FB]
        for p in range(Q):
            term = stat_flux(stat_ref, p, q) * field
            acc[p] = term if acc[p] is None else acc[p] + term
    nothing = jnp.zeros((8, LANES), F32)
    for p in range(Q):
        lanes = group(place(p))
        turned = fill_z(lanes, [acc[p][0:8]] * 4, acc[p][8:16], rm_ref, ru_ref, s.rzh, s.rzl)
        finish_z(lanes, turned, nothing, s.rzh, s.rzl)


def place_of(nbr_ref, columns):
    here = jnp.broadcast_to(nbr_ref[0:1, LANES : 2 * LANES] >> 8, (8, LANES))
    return (here // columns & 1) == 0, (here & 1) == 0


def pack(current_ref, other, stat_ref, msg_refs, even):
    blocks = []
    for p in range(Q):
        for r in range(3):
            blocks.append(current_ref[p, 8 * r : 8 * r + 8, 0:LANES])
    for p in range(Q):
        value = other(p)
        for r in range(3):
            blocks.append(value[8 * r : 8 * r + 8])
    if stat_ref is not None:
        blocks += [stat_ref[n] for n in range(STATIC)]
    while len(blocks) % 4:
        blocks.append(jnp.zeros((8, LANES), F32))
    for g in range(len(blocks) // 4):
        value = transpose_quarters(blocks[4 * g : 4 * g + 4])
        msg_refs[0][g] = jnp.where(even[0], value[1], value[0])
        msg_refs[1][g] = jnp.where(even[0], value[0], value[1])
        msg_refs[2][g] = jnp.where(even[1], value[2], value[3])
        msg_refs[3][g] = jnp.where(even[1], value[3], value[2])


def unpack(msg_refs, first, last, store, even):
    for g in range(first // 4, -(-last // 4)):
        one, two, three, last_one = (msg_refs[k][g] for k in range(4))
        four = [
            jnp.where(even[0], two, one),
            jnp.where(even[0], one, two),
            jnp.where(even[1], three, last_one),
            jnp.where(even[1], last_one, three),
        ]
        for m, value in enumerate(transpose_quarters(four)):
            if first <= 4 * g + m < last:
                store(4 * g + m - first, value)


def even_half(s, r, fine, dofs_ref, o, stat_ref):
    stars = [own_star(r.star, lg) for lg in range(2)]
    predict(dofs_ref, stars, r.wt, s.term, s.moved, [(s.cur, FIRST), (o.curo, SECOND)])
    for p in range(Q):
        o.curb[p] = s.cur[p, :, 0:LANES]
        o.base[p] = dofs_ref[p, :, LANES : 2 * LANES]
    spread_and_project(s.cur, r.wb, s)
    change_of([dofs_ref.at[:, :, 0:LANES]], [o.part0], r, s, [0])
    lead = fine[:, 0:LANES] > 0.5
    pack(
        s.cur,
        lambda p: jnp.where(lead, o.part0[p], o.curo[p, :, 0:LANES]),
        stat_ref,
        [o[key] for key in SENT],
        r.even,
    )


def rest_half(s, r, o):
    change_of([None, r.base], [None, o.part1], r, s, [1])
    project_remote(r.curb, r.wb, o.rtable2)
    predict(o.part1, [own_star(r.star, 1)], r.wt, s.term1, s.pmoved1, [(o.ahead, FIRST)])


def odd_half(s, r, fine, ghost_ref, outs):
    def keep_table(n, value):
        s.gfield[n // 3, 8 * (n % 3) : 8 * (n % 3) + 8, :] = value

    def keep_other(n, value):
        s.dofs[n // 3, 8 * (n % 3) : 8 * (n % 3) + 8, LANES : 2 * LANES] = value

    recv_refs = [r[key] for key in GOT]
    s.rzh[96:128] = jnp.zeros((32, s.rzh.shape[1]), BF16)
    s.rzl[96:128] = jnp.zeros((32, s.rzl.shape[1]), BF16)
    unpack(recv_refs, 0, 27, keep_table, r.even)
    unpack(recv_refs, 27, 54, keep_other, r.even)
    project_remote(s.gfield, r.wb, s.rtable)
    remote_z(s.rtable, r.stat, r.rhot, r.rm, r.ru, s, lambda p: 2 * p)
    remote_z(r.rtable2, ghost_ref, s.rhot2, s.rm2, s.ru2, s, lambda p: 2 * p + 1)

    def first_store(p, total):
        value = s.dofs[p, :, LANES : 2 * LANES]
        s.gfield[p] = value
        s.dofs[p, :, LANES : 2 * LANES] = value - total[:, LANES : 2 * LANES]
        s.dofs[p, :, 0:LANES] = r.part0[p] - total[:, 0:LANES]

    lift(r.wl, s.rzh, s.rzl, 2 * LANES, first_store)
    ghost_fine = ghost_ref[41, 5:6] > 0.5
    stars = [own_star(r.star, 0), stat_star(ghost_ref)]
    predict(s.dofs, stars, r.wt, s.term, s.moved, [(s.edge, FIRST)])
    for p in range(Q):
        s.cur[p, :, 0:LANES] = jnp.where(fine[:, 0:LANES] > 0.5, s.edge[p, :, 0:LANES], r.curo[p, :, 0:LANES])
        s.cur[p, :, LANES:256] = jnp.where(fine[:, LANES:256] > 0.5, r.ahead[p], r.curo[p, :, LANES:256])
        s.gfield[p] = jnp.where(ghost_fine, s.edge[p, :, LANES:256], s.gfield[p])
    project_remote(s.gfield, r.wb, s.rtable)
    spread_and_project(s.cur, r.wb, s)
    remote_z(s.rtable, r.stat, r.rhot, r.rm, r.ru, s, lambda p: p)

    def second_store(p, total):
        s.dofs[p, :, 0:LANES] = s.dofs[p, :, 0:LANES] - total

    lift(r.wl, s.rzh, s.rzl, LANES, second_store)
    change_of([s.dofs.at[:, :, 0:LANES], r.part1], outs, r, s, [0, 1])


FIELD = ((Q, B, LANES), F32)
SPREAD = dict(
    moved0=((Q, 3 * B, LANES), F32),
    face0=((4, Q, FB, LANES), F32),
)
KEPT = dict(
    moved1=((Q, 3 * B, LANES), F32),
    face1=((4, Q, FB, LANES), F32),
    table=((2 * Q * FB, 1024), BF16),
)
CHANGE = dict(
    across=((4, Q * FB, LANES), F32),
    zh=((KZ, Q * 256), BF16),
    zl=((KZ, Q * 256), BF16),
)
PREDICT = dict(
    dofs=((Q, B, 256), F32),
    cur=((Q, B, 256), F32),
    term=((Q, B, 256), F32),
    moved=((Q, 3 * B, 256), F32),
)
REMOTE = dict(
    gfield=FIELD,
    edge=((Q, B, 256), F32),
    rtable=((2 * Q * FB, 512), BF16),
    rzh=((KZ, Q * 256), BF16),
    rzl=((KZ, Q * 256), BF16),
)
EVEN = dict(part0=FIELD, base=FIELD, curb=FIELD, curo=((Q, B, 256), F32), **KEPT)
GHOST_MASKS = dict(rhot2=((512, LANES), BF16), rm2=((6, FB, LANES), BF16), ru2=((3, 8, LANES), F32))
STAT = ((STATIC, 8, LANES), F32)
LOADED = ("star", "fluxl", "fluxn", "nbr", "kind", "cluster")
SMALL = ("time", "volume", "project", "rotate", "lift")


def masks(lg):
    shapes = dict(
        hot=((1024, 512), BF16), tm=((6, FB, LANES), BF16), um=((3, 8, LANES), F32),
        fpl=((Q * Q, 8, LANES), F32), fpn=((Q * Q, 8, LANES), F32),
    )
    return {key + str(lg): value for key, value in shapes.items()}


def messages(blocks):
    return {key: ((blocks // 4, 8, LANES), F32) for key in SENT}


def call(kernel, name, ins, outs, scratch, inputs, columns, hbm=False, flops=0):
    def body(*refs):
        n, m = len(ins), len(outs)
        r = Bag(zip(ins, refs[:n]))
        o = Bag(zip(outs, refs[n : n + m]))
        s = Bag(zip(scratch, refs[n + m : n + m + len(scratch)]))
        if hbm:
            sems = refs[-1]
            copies = {}
            for k, key in enumerate((*SMALL, "nbr", "kind", "cluster", "dofs", "star", "fluxn", "fluxl")):
                to = o[key] if key in LOADED else s[key + "_in"]
                copies[key] = pltpu.make_async_copy(r[key], to, sems.at[k])
                copies[key].start()
            r = Bag({key: o[key] if key in LOADED else s[key + "_in"] for key in ins})
            kernel(r, o, s, lambda *keys: [copies[key].wait() for key in keys], columns)
        else:
            r.even = place_of(r.nbr, columns)
            kernel(r, o, s)

    shapes = [pltpu.VMEM(*scratch[key]) for key in scratch]
    if hbm:
        shapes.append(pltpu.SemaphoreType.DMA((len(ins),)))
    space = pltpu.HBM if hbm else pltpu.VMEM
    got = pl.pallas_call(
        body,
        out_shape=[jax.ShapeDtypeStruct(*outs[key]) for key in outs],
        in_specs=[pl.BlockSpec(memory_space=space)] * len(ins),
        out_specs=[pl.BlockSpec(memory_space=pltpu.VMEM)] * len(outs),
        scratch_shapes=shapes,
        compiler_params=pltpu.CompilerParams(vmem_limit_bytes=24 << 20),
        cost_estimate=pl.CostEstimate(flops=flops, bytes_accessed=1 << 20, transcendentals=0),
        name=name,
    )(*(pltpu.with_memory_space_constraint(inputs[key], space) if hbm else inputs[key] for key in ins))
    return dict(zip(outs, got))


def fine_of(cluster_ref):
    return (cluster_ref[...] == 0).astype(F32)


def first_kernel(r, o, s, wait, columns):
    wait("time")
    prepare_predictor(r.time, o.wt, s.ptmp)
    wait("volume", "project", "rotate", "lift")
    prepare(r.volume, r.project, r.rotate, r.lift, o.wb, o.wl, s.ptmp, s.pturn, s.pbig)
    wait("nbr", "kind", "cluster")
    build_onehot(r.nbr, r.kind, o, [0])
    wait("dofs")
    for p in range(Q):
        s.dofs[p, 0:20, 0:256] = r.dofs[p]
        s.dofs[p, 20:B, 0:256] = jnp.zeros((B - 20, 256), F32)
    wait("star", "fluxn", "fluxl")
    keep_rows(r.fluxl, 0, o.fpl0)
    keep_rows(r.fluxn, 0, o.fpn0)
    describe(r.nbr, r.kind, r.cluster, r.star, r.fluxn, o.stat)
    r = Bag(r, wt=o.wt, wb=o.wb, wl=o.wl, even=place_of(r.nbr, columns))
    even_half(s | o, r, fine_of(r.cluster), s.dofs, o, o.stat)


def first_rest(r, o, s):
    build_onehot(r.nbr, r.kind, o, [1])
    keep_rows(r.fluxl, 1, o.fpl1)
    keep_rows(r.fluxn, 1, o.fpn1)
    build_remote(r.stat, o.rhot, o.rm, o.ru)
    rest_half(r | o | s, r, o)


def middle_kernel(r, o, s):
    def keep(n, value):
        o.ghost[n] = value

    unpack([r[key] for key in GOT], 54, 54 + STATIC, keep, r.even)
    build_remote(o.ghost, o.rhot2, o.rm2, o.ru2)
    fine = fine_of(r.cluster)
    s = r | s | o
    odd_half(s, r, fine, o.ghost, [s.next.at[:, :, group(lg)] for lg in range(2)])
    even_half(s, r, fine, s.next, o, None)


def second_rest(r, o, s):
    rest_half(r | o | s, r, o)


def last_kernel(r, o, s):
    s = r | s
    odd_half(s, r, fine_of(r.cluster), r.ghost, [s.next.at[:, :, group(lg)] for lg in range(2)])
    for p in range(Q):
        o.out[p] = s.next[p, 0:20, :]


def trade(got):
    out = {}
    for m, (axis, start) in enumerate((("px", 0), ("px", 1), ("py", 1), ("py", 0))):
        count = lax.axis_size(axis)
        pairs = []
        for low in range(start, count - 1, 2):
            pairs += [(low, low + 1), (low + 1, low)]
        out[GOT[m]] = lax.ppermute(got[SENT[m]], axis, pairs)
    return out


def per_device(dofs, star, flux_local, flux_neigh, time_stiff, volume_stiff, face_project, face_rotate, face_lift, cluster, neighbors, face_kind):
    columns = lax.axis_size("py")
    inputs = dict(
        dofs=dofs, star=star.transpose(1, 2, 0, 3), fluxl=flux_local.transpose(1, 2, 0, 3),
        fluxn=flux_neigh.transpose(1, 2, 0, 3), time=time_stiff, volume=volume_stiff,
        project=face_project.transpose(1, 0, 2), rotate=face_rotate.transpose(1, 0, 2), lift=face_lift.transpose(2, 0, 1),
        cluster=cluster.reshape(1, 256), nbr=neighbors, kind=face_kind,
    )
    first = {
        **{key: (inputs[key].shape, inputs[key].dtype) for key in LOADED},
        "wt": ((80, 80), BF16),
        "wb": ((144, 80), BF16),
        "wl": ((64, KZ), BF16),
        "stat": STAT,
        **masks(0),
        **EVEN,
        **messages(96),
    }
    scratch = {
        **PREDICT, **SPREAD, **CHANGE, "ptmp": ((144, LANES), F32), "pturn": ((LANES, LANES), F32), "pbig": ((256, LANES), F32),
        **{key + "_in": (inputs[key].shape, inputs[key].dtype) for key in (*SMALL, "dofs")},
    }
    alone = dict(**CHANGE, term1=FIELD, pmoved1=((Q, 3 * B, LANES), F32))
    weights = ["star", "fluxl", "fluxn", "wt", "wb", "wl", "nbr"]
    rest = {"part1": FIELD, "ahead": FIELD, "rtable2": ((2 * Q * FB, 512), BF16)}
    state = ["part0", "part1", "ahead", "rtable2", "curo", *GOT]
    odd = weights + ["cluster", "stat", *masks(0), *masks(1), "rhot", "rm", "ru"] + state
    inputs |= call(first_kernel, "first", list(inputs), first, scratch, inputs, columns, hbm=True)
    inputs |= trade(inputs)
    inputs |= call(
        first_rest, "first_rest", weights + ["kind", "stat", "base", "curb", *KEPT],
        {**rest, **masks(1), "rhot": ((512, LANES), BF16), "rm": ((6, FB, LANES), BF16), "ru": ((3, 8, LANES), F32)},
        alone, inputs, columns, flops=10**9,
    )
    both = {**PREDICT, **SPREAD, **CHANGE, **REMOTE, "next": ((Q, B, 256), F32)}
    inputs |= call(
        middle_kernel, "middle", odd, {"ghost": STAT, **GHOST_MASKS, **EVEN, **messages(56)}, both, inputs, columns,
    )
    inputs |= trade(inputs)
    inputs |= call(
        second_rest, "second_rest", weights + ["base", "curb", *masks(1), *KEPT], rest, alone, inputs, columns,
        flops=10**9,
    )
    got = call(
        last_kernel, "last", odd + ["ghost", *GHOST_MASKS], {"out": ((Q, 20, 256), F32)}, {**both, **KEPT}, inputs, columns,
    )
    return got["out"]


def solution(mesh):
    cells = ("px", "py")
    placed = (
        P(None, None, cells),
        P(None, None, None, cells),
        P(None, None, None, cells),
        P(None, None, None, cells),
        P(),
        P(),
        P(),
        P(),
        P(),
        P(cells),
        P(None, cells),
        P(None, cells),
    )
    return jax.shard_map(
        per_device,
        mesh=mesh,
        in_specs=placed,
        out_specs=P(None, None, cells),
        check_vma=False,
    )
```

```python
import math
from functools import partial

import jax
import jax.numpy as jnp
from jax import lax
from jax.experimental import pallas as pl
from jax.experimental.pallas import tpu as pltpu
from jax.sharding import PartitionSpec as P

ORDER = 4
NS = 32
Q = 9
B = 24
FB = 16
LANES = 128
TABLE = 96
KZ = 160
STATIC = 42
F32 = jnp.float32
BF16 = jnp.bfloat16
HIGHEST = lax.Precision.HIGHEST
STEP = 0.4
SENT = ("m0", "m1", "m2", "m3")
GOT = ("r0", "r1", "r2", "r3")


class Bag(dict):
    __getattr__ = dict.__getitem__
    __setattr__ = dict.__setitem__

    def __or__(self, other):
        return Bag({**self, **other})

    def pick(self, name, lg):
        return self[name + str(lg)]


def series(start, stop):
    return [
        (stop ** (power + 1) - start ** (power + 1)) / math.factorial(power + 1)
        for power in range(ORDER)
    ]


FIRST = series(0.0, STEP)
SECOND = series(STEP, 2.0 * STEP)


def halves(x):
    high = x.astype(BF16)
    return high, (x - high.astype(F32)).astype(BF16)


def stacked(x):
    high = x.astype(BF16).astype(F32)
    rest = jnp.zeros((8, x.shape[1]), F32)
    return jnp.concatenate([high, x - high, high, rest], axis=0).astype(BF16)


def mm(a, b):
    return jnp.dot(a, b, preferred_element_type=F32)


def group(lg):
    return pl.ds(lg * LANES, LANES)


def transpose_quarters(four):
    quarter = lax.broadcasted_iota(jnp.int32, (8, LANES), 1) // NS
    out = []
    for k in range(4):
        total = None
        for m in range(4):
            shift = (NS * (m - k)) % LANES
            moved = pltpu.roll(four[m], shift, 1) if shift else four[m]
            total = moved if total is None else jnp.where(quarter == m, moved, total)
        out.append(total)
    return out


def widened(block):
    high = block.astype(BF16).astype(F32)
    return (high + pltpu.roll(high, B, 1) + pltpu.roll(block - high, 2 * B, 1)).astype(BF16)


def prepare_predictor(time_ref, wt_ref, tmp_ref):
    tmp_ref[...] = jnp.zeros_like(tmp_ref)
    for d in range(3):
        tmp_ref[B * d : B * d + 20, 0:20] = -time_ref[d]
    wt_ref[...] = widened(tmp_ref[0:80])[:, 0:80]


def prepare(volume_ref, project_ref, rotate_ref, lift_ref, wb_ref, wl_ref, tmp_ref, turn_ref, big_ref):
    for d in range(3):
        tmp_ref[B * d : B * d + 20, 0:20] = volume_ref[d]
    for j in range(4):
        at = 3 * B + FB * j
        tmp_ref[at : at + 8, 0:20] = project_ref[0:8, j, :]
        for r in range(4):
            tmp_ref[at + 8 + r : at + 9 + r, 0:20] = project_ref[8:9, j, :]
            tmp_ref[at + 12 + r : at + 13 + r, 0:20] = project_ref[9:10, j, :]
    wb_ref[...] = widened(tmp_ref[...])[:, 0:80]
    turn_ref[...] = jnp.zeros_like(turn_ref)
    for t in range(3):
        turn_ref[0:10, FB * t : FB * t + 10] = rotate_ref[:, t, :]
    rows = lax.broadcasted_iota(jnp.int32, (10, 10), 0)
    cols = lax.broadcasted_iota(jnp.int32, (10, 10), 1)
    turn_ref[0:10, 3 * FB : 3 * FB + 10] = (rows == cols).astype(F32)
    turns = turn_ref[...].T[0:64, 0:16]
    big_ref[...] = jnp.zeros_like(big_ref)
    for i in range(4):
        big_ref[0:10, 32 * i : 32 * i + 20] = lift_ref[:, i, :]
    both = jnp.dot(turns, big_ref[0:16], precision=HIGHEST, preferred_element_type=F32)
    big_ref[0:16] = jnp.zeros((16, LANES), F32)
    for i in range(4):
        mine = pltpu.roll(both, LANES - 32 * i, 1) if i else both
        for t in range(4):
            at = (((i // 2) * 3 + t) if t < 3 else 6 + i // 2) * FB + 8 * (i % 2)
            big_ref[at : at + 8] = mine[FB * t : FB * t + 8]
            for g in (8, 9):
                at = 128 + 8 * t + 4 * (g - 8) + i
                big_ref[at : at + 1] = mine[FB * t + g : FB * t + g + 1]
    total = big_ref[...].T[0:32, 0:KZ]
    high = total.astype(BF16).astype(F32)
    wl_ref[...] = jnp.concatenate([high, total - high], axis=0).astype(BF16)


def describe(nbr_ref, kind_ref, cluster_ref, star_ref, fluxn_ref, stat_ref):
    lanes = pl.ds(0, LANES)
    here = nbr_ref[0:1, LANES : 2 * LANES] >> 8
    remote = []
    for i in range(4):
        nbr = nbr_ref[i : i + 1, lanes]
        remote.append((nbr >= 0) & ((nbr >> 8) != here))
    spot = jnp.full((1, LANES), -1, jnp.int32)
    side = jnp.full((1, LANES), -1, jnp.int32)
    turn = jnp.full((1, LANES), -1, jnp.int32)
    face = jnp.full((1, LANES), -1, jnp.int32)
    for i in range(4):
        kind = kind_ref[i : i + 1, lanes]
        spot = jnp.where(remote[i], nbr_ref[i : i + 1, lanes] & (NS - 1), spot)
        side_i = (kind >= 3).astype(jnp.int32) + (kind >= 6).astype(jnp.int32) + (kind >= 9).astype(jnp.int32)
        side = jnp.where(remote[i], side_i, side)
        turn = jnp.where(remote[i], kind - 3 * side_i, turn)
        face = jnp.where(remote[i], i, face)
    weight = [jnp.where(r, 1.0, 0.0).astype(F32) for r in remote]
    stat_ref[27 + 3] = jnp.zeros((8, LANES), F32)
    for d in range(3):
        for p in range(Q):
            at = d * Q + p
            stat_ref[at] = star_ref[p, 0:8, d, lanes]
            stat_ref[27 + at // 8, at % 8 : at % 8 + 1] = star_ref[p, 8, d : d + 1, lanes]
    stat_ref[41] = jnp.zeros((8, LANES), F32)
    for p in range(Q):
        total, last = None, None
        for i in range(4):
            term = fluxn_ref[p, 0:8, i, lanes] * weight[i]
            term_last = fluxn_ref[p, 8, i : i + 1, lanes] * weight[i]
            total = term if total is None else total + term
            last = term_last if last is None else last + term_last
        stat_ref[31 + p] = total
        stat_ref[40 + p // 8, p % 8 : p % 8 + 1] = last
    fine = (cluster_ref[0:1, lanes] == 0).astype(F32)
    for row, value in enumerate((spot.astype(F32), side.astype(F32), turn.astype(F32), face.astype(F32), fine)):
        stat_ref[41, row + 1 : row + 2] = value


def stat_star(stat_ref):
    def at(d, p, q):
        n = d * Q + p
        return stat_ref[n, q : q + 1] if q < 8 else stat_ref[27 + n // 8, n % 8 : n % 8 + 1]

    return at


def stat_flux(stat_ref, p, q):
    return stat_ref[31 + p, q : q + 1] if q < 8 else stat_ref[40 + p // 8, p % 8 : p % 8 + 1]


def own_star(star_ref, lg):
    return lambda d, p, q: star_ref[p, q, d : d + 1, group(lg)]


def apply_star(star, moved_ref, lanes):
    acc = [None] * Q
    for q in range(Q):
        for d in range(3):
            field = moved_ref[q, B * d : B * d + B, lanes]
            for p in range(Q):
                term = star(d, p, q) * field
                acc[p] = term if acc[p] is None else acc[p] + term
    return acc


def predict(dofs_ref, stars, wt_ref, term_ref, moved_ref, outs):
    width = LANES * len(stars)
    for power in range(ORDER - 1):
        source = term_ref if power else dofs_ref
        for q in range(Q):
            moved_ref[q, 0 : 3 * B, 0:width] = mm(wt_ref[...], stacked(source[q, :, 0:width]))[0 : 3 * B]
        for lg, star in enumerate(stars):
            acc = apply_star(star, moved_ref, group(lg))
            for p in range(Q):
                if power < ORDER - 2:
                    term_ref[p, :, group(lg)] = acc[p]
                for out_ref, coeffs in outs:
                    before = out_ref[p, :, group(lg)] if power else coeffs[0] * dofs_ref[p, :, group(lg)]
                    out_ref[p, :, group(lg)] = before + coeffs[power + 1] * acc[p]


def keep_masks(test, pair_ref, last_ref):
    for t in range(3):
        mask = [jnp.where(test(i, t), 1.0, 0.0).astype(F32) for i in range(4)]
        for pair in range(2):
            two = [jnp.broadcast_to(mask[2 * pair + n], (8, LANES)) for n in range(2)]
            pair_ref[pair * 3 + t] = jnp.concatenate(two, axis=0).astype(BF16)
        last_ref[t] = by_face(mask)


def by_face(four):
    which = lax.broadcasted_iota(jnp.int32, (8, LANES), 0) & 3
    total = jnp.broadcast_to(four[0], (8, LANES))
    for i in range(1, 4):
        total = jnp.where(which == i, four[i], total)
    return total


def keep_rows(flux_ref, lg, rows_ref):
    for p in range(Q):
        for q in range(Q):
            tile = flux_ref[p, q, :, group(lg)]
            rows_ref[p * Q + q, 0:4] = tile
            rows_ref[p * Q + q, 4:8] = tile


def fill_z(lanes, mains, last, pair_ref, last_ref, zh_ref, zl_ref):
    for pair in range(2):
        high, low = halves(jnp.concatenate(mains[2 * pair : 2 * pair + 2], axis=0))
        for t in range(3):
            at = pl.ds((pair * 3 + t) * FB, FB)
            zh_ref[at, lanes] = high * pair_ref[pair * 3 + t]
            zl_ref[at, lanes] = low * pair_ref[pair * 3 + t]
    return [last * last_ref[t] for t in range(3)]


def finish_z(lanes, turned, local, zh_ref, zl_ref):
    for n, two in enumerate(((turned[0], turned[1]), (turned[2], local))):
        high, low = halves(jnp.concatenate(two, axis=0))
        zh_ref[128 + n * FB : 128 + (n + 1) * FB, lanes] = high
        zl_ref[128 + n * FB : 128 + (n + 1) * FB, lanes] = low


def lift(wl_ref, zh_ref, zl_ref, width, store):
    for start in range(0, Q * width, 2 * LANES):
        stop = min(start + 2 * LANES, Q * width)
        lifted = mm(wl_ref[...], zh_ref[:, start:stop])
        rest = mm(wl_ref[0:32], zl_ref[:, start:stop])
        total = lifted[0:B] + lifted[32 : 32 + B] + rest[0:B]
        for p in range(start // width, stop // width):
            store(p, total[:, p * width - start : (p + 1) * width - start])


def build_onehot(nbr_ref, kind_ref, s, groups):
    index = lax.broadcasted_iota(jnp.int32, (256, LANES), 0)
    here = nbr_ref[0:1, LANES : 2 * LANES] >> 8
    for lg in groups:
        turns = []
        for i in range(4):
            nbr = nbr_ref[i : i + 1, group(lg)]
            kind = kind_ref[i : i + 1, group(lg)]
            local = (nbr >= 0) & ((nbr >> 8) == here)
            side = (kind >= 3).astype(jnp.int32) + (kind >= 6).astype(jnp.int32) + (kind >= 9).astype(jnp.int32)
            turn = kind - 3 * side
            for j in range(4):
                pick = jnp.where(local & (side == j), nbr & 255, -1)
                hot = jnp.where(index == pick, 1.0, 0.0).astype(BF16)
                s.pick("hot", lg)[j * 256 : (j + 1) * 256, group(i)] = hot
            turns.append(turn)
        keep_masks(lambda i, t: turns[i] == t, s.pick("tm", lg), s.pick("um", lg))


def spread_and_project(cur_ref, wb_ref, s):
    for q in range(Q):
        got = mm(wb_ref[...], stacked(cur_ref[q, :, 0:256]))
        for lg in range(2):
            half = got[:, lg * LANES : (lg + 1) * LANES]
            s.pick("moved", lg)[q] = half[0 : 3 * B]
            for j in range(4):
                s.pick("face", lg)[j, q] = half[3 * B + FB * j : 3 * B + FB * (j + 1)]
    for lg in range(2):
        face = s.pick("face", lg)
        for j in range(4):
            blocks = [face[j, q, 0:8] for q in range(Q)]
            blocks += [by_face([face[j, min(q + n, Q - 1), 8:16] for n in range(4)]) for q in range(0, Q, 4)]
            cols = group(2 * j + lg)
            for n in range(0, 12, 2):
                high, low = halves(jnp.concatenate(blocks[n : n + 2], axis=0))
                s.table[8 * n : 8 * n + 16, cols] = high
                s.table[TABLE + 8 * n : TABLE + 8 * n + 16, cols] = low


def change_of(base, out, r, s, groups, finish=None):
    def keep(p, lg, value):
        out[lg][p] = value

    finish = finish or keep
    for lg in groups:
        for pair in range(2):
            cols = pl.ds(2 * pair * LANES, 2 * LANES)
            got = mm(s.table[...], s.pick("hot", lg)[:, cols])
            total = got[0:TABLE] + got[TABLE : 2 * TABLE]
            for half in range(2):
                s.across[2 * pair + half] = total[:, half * LANES : (half + 1) * LANES]
        face, across = s.pick("face", lg), s.across

        def last_own(q):
            return by_face([face[k, q, 8:16] for k in range(4)])

        def last_across(q):
            at = Q * 8 + q // 4 * 8
            found = [across[k, at : at + 8] for k in range(4)]
            if q < 8:
                found = [pltpu.roll(f, (k - q % 4) % 8, 0) if k != q % 4 else f for k, f in enumerate(found)]
            return by_face(found)

        sources = (
            (r.fluxl, s.pick("fpl", lg), lambda i, q: face[i, q, 0:8], last_own),
            (r.fluxn, s.pick("fpn", lg), lambda i, q: across[i, q * 8 : (q + 1) * 8], last_across),
        )
        got = []
        for flux_ref, rows_ref, main, last in sources:
            sums = []
            for i in range(5):
                acc = [None] * Q
                for q in range(Q):
                    value = main(i, q) if i < 4 else last(q)
                    for p in range(Q):
                        scale = flux_ref[p, q, i : i + 1, group(lg)] if i < 4 else rows_ref[p * Q + q]
                        term = scale * value
                        acc[p] = term if acc[p] is None else acc[p] + term
                sums.append(acc)
            got.append(sums)
        local, other = got
        for p in range(Q):
            mains = [other[i][p] for i in range(4)]
            at_lg = group(p * len(groups) + groups.index(lg))
            turned = fill_z(at_lg, mains, other[4][p], s.pick("tm", lg), s.pick("um", lg), s.zh, s.zl)
            for pair in range(2):
                high, low = halves(jnp.concatenate([local[2 * pair][p], local[2 * pair + 1][p]], axis=0))
                s.zh[96 + pair * FB : 96 + (pair + 1) * FB, at_lg] = high
                s.zl[96 + pair * FB : 96 + (pair + 1) * FB, at_lg] = low
            finish_z(at_lg, turned, local[4][p], s.zh, s.zl)
        acc = apply_star(own_star(r.star, lg), s.pick("moved", lg), group(0))
        for p in range(Q):
            out[lg][p] = base[lg][p] + acc[p]

    def store(p, total):
        for n, lg in enumerate(groups):
            finish(p, lg, out[lg][p] - total[:, n * LANES : (n + 1) * LANES])

    lift(r.wl, s.zh, s.zl, len(groups) * LANES, store)


def build_remote(stat_ref, rhot_ref, rm_ref, ru_ref):
    index = lax.broadcasted_iota(jnp.int32, (LANES, LANES), 0).astype(F32)
    spot, side, turn, face = (stat_ref[41, r : r + 1] for r in range(1, 5))
    segment = (lax.broadcasted_iota(jnp.int32, (1, LANES), 1) // NS * NS).astype(F32)
    spot = spot + segment
    for j in range(4):
        pick = jnp.where(side == float(j), spot, -1.0)
        rhot_ref[j * LANES : (j + 1) * LANES] = jnp.where(index == pick, 1.0, 0.0).astype(BF16)
    keep_masks(lambda i, t: (face == float(i)) & (turn == float(t)), rm_ref, ru_ref)


def project_remote(field_ref, wb_ref, table_ref):
    weights = wb_ref[3 * B - 8 :]
    fields = [stacked(field_ref[q]) for q in range(Q)]
    for start in range(0, Q, 2):
        two = fields[start : start + 2]
        got = mm(weights, jnp.concatenate(two, axis=1))
        for n in range(len(two)):
            q = start + n
            for j in range(4):
                high, low = halves(got[8 + FB * j : 8 + FB * (j + 1), n * LANES : (n + 1) * LANES])
                table_ref[q * FB : (q + 1) * FB, j * LANES : (j + 1) * LANES] = high
                table_ref[(Q + q) * FB : (Q + q + 1) * FB, j * LANES : (j + 1) * LANES] = low


def remote_z(table_ref, stat_ref, rhot_ref, rm_ref, ru_ref, s, place):
    rows = Q * FB
    got = mm(table_ref[...], rhot_ref[...])
    across = got[0:rows] + got[rows : 2 * rows]
    acc = [None] * Q
    for q in range(Q):
        field = across[q * FB : (q + 1) * FB]
        for p in range(Q):
            term = stat_flux(stat_ref, p, q) * field
            acc[p] = term if acc[p] is None else acc[p] + term
    nothing = jnp.zeros((8, LANES), F32)
    for p in range(Q):
        lanes = group(place(p))
        turned = fill_z(lanes, [acc[p][0:8]] * 4, acc[p][8:16], rm_ref, ru_ref, s.rzh, s.rzl)
        finish_z(lanes, turned, nothing, s.rzh, s.rzl)


def place_of(nbr_ref, columns):
    here = jnp.broadcast_to(nbr_ref[0:1, LANES : 2 * LANES] >> 8, (8, LANES))
    return (here // columns & 1) == 0, (here & 1) == 0


def pack(current_ref, other, stat_ref, msg_refs, even):
    blocks = []
    for p in range(Q):
        for r in range(3):
            blocks.append(current_ref[p, 8 * r : 8 * r + 8, 0:LANES])
    for p in range(Q):
        value = other(p)
        for r in range(3):
            blocks.append(value[8 * r : 8 * r + 8])
    if stat_ref is not None:
        blocks += [stat_ref[n] for n in range(STATIC)]
    while len(blocks) % 4:
        blocks.append(jnp.zeros((8, LANES), F32))
    for g in range(len(blocks) // 4):
        value = transpose_quarters(blocks[4 * g : 4 * g + 4])
        msg_refs[0][g] = jnp.where(even[0], value[1], value[0])
        msg_refs[1][g] = jnp.where(even[0], value[0], value[1])
        msg_refs[2][g] = jnp.where(even[1], value[2], value[3])
        msg_refs[3][g] = jnp.where(even[1], value[3], value[2])


def unpack(msg_refs, first, last, store, even):
    for g in range(first // 4, -(-last // 4)):
        one, two, three, last_one = (msg_refs[k][g] for k in range(4))
        four = [
            jnp.where(even[0], two, one),
            jnp.where(even[0], one, two),
            jnp.where(even[1], three, last_one),
            jnp.where(even[1], last_one, three),
        ]
        for m, value in enumerate(transpose_quarters(four)):
            if first <= 4 * g + m < last:
                store(4 * g + m - first, value)


def even_half(s, r, fine, dofs_ref, o, stat_ref):
    stars = [own_star(r.star, lg) for lg in range(2)]
    predict(dofs_ref, stars, r.wt, s.term, s.moved, [(s.cur, FIRST), (o.curo, SECOND)])
    for p in range(Q):
        o.curb[p] = s.cur[p, :, 0:LANES]
        o.base[p] = dofs_ref[p, :, LANES : 2 * LANES]
    spread_and_project(s.cur, r.wb, s)
    change_of([dofs_ref.at[:, :, 0:LANES]], [o.part0], r, s, [0])
    lead = fine[:, 0:LANES] > 0.5
    pack(
        s.cur,
        lambda p: jnp.where(lead, o.part0[p], o.curo[p, :, 0:LANES]),
        stat_ref,
        [o[key] for key in SENT],
        r.even,
    )


def rest_half(s, r, o):
    change_of([None, r.base], [None, o.part1], r, s, [1])
    project_remote(r.curb, r.wb, o.rtable2)
    predict(o.part1, [own_star(r.star, 1)], r.wt, s.term1, s.pmoved1, [(o.ahead, FIRST)])


def odd_half(s, r, fine, ghost_ref, outs, finish=None):
    def keep_table(n, value):
        s.gfield[n // 3, 8 * (n % 3) : 8 * (n % 3) + 8, :] = value

    def keep_other(n, value):
        s.dofs[n // 3, 8 * (n % 3) : 8 * (n % 3) + 8, LANES : 2 * LANES] = value

    recv_refs = [r[key] for key in GOT]
    s.rzh[96:128] = jnp.zeros((32, s.rzh.shape[1]), BF16)
    s.rzl[96:128] = jnp.zeros((32, s.rzl.shape[1]), BF16)
    unpack(recv_refs, 0, 27, keep_table, r.even)
    unpack(recv_refs, 27, 54, keep_other, r.even)
    project_remote(s.gfield, r.wb, s.rtable)
    remote_z(s.rtable, r.stat, r.rhot, r.rm, r.ru, s, lambda p: 2 * p)
    remote_z(r.rtable2, ghost_ref, s.rhot2, s.rm2, s.ru2, s, lambda p: 2 * p + 1)

    def first_store(p, total):
        value = s.dofs[p, :, LANES : 2 * LANES]
        s.gfield[p] = value
        s.dofs[p, :, LANES : 2 * LANES] = value - total[:, LANES : 2 * LANES]
        s.dofs[p, :, 0:LANES] = r.part0[p] - total[:, 0:LANES]

    lift(r.wl, s.rzh, s.rzl, 2 * LANES, first_store)
    ghost_fine = ghost_ref[41, 5:6] > 0.5
    stars = [own_star(r.star, 0), stat_star(ghost_ref)]
    predict(s.dofs, stars, r.wt, s.term, s.moved, [(s.edge, FIRST)])
    for p in range(Q):
        s.cur[p, :, 0:LANES] = jnp.where(fine[:, 0:LANES] > 0.5, s.edge[p, :, 0:LANES], r.curo[p, :, 0:LANES])
        s.cur[p, :, LANES:256] = jnp.where(fine[:, LANES:256] > 0.5, r.ahead[p], r.curo[p, :, LANES:256])
        s.gfield[p] = jnp.where(ghost_fine, s.edge[p, :, LANES:256], s.gfield[p])
    project_remote(s.gfield, r.wb, s.rtable)
    spread_and_project(s.cur, r.wb, s)
    remote_z(s.rtable, r.stat, r.rhot, r.rm, r.ru, s, lambda p: p)

    def second_store(p, total):
        s.dofs[p, :, 0:LANES] = s.dofs[p, :, 0:LANES] - total

    lift(r.wl, s.rzh, s.rzl, LANES, second_store)
    change_of([s.dofs.at[:, :, 0:LANES], r.part1], outs, r, s, [0, 1], finish)


FIELD = ((Q, B, LANES), F32)
SPREAD = dict(
    moved0=((Q, 3 * B, LANES), F32),
    face0=((4, Q, FB, LANES), F32),
)
KEPT = dict(
    moved1=((Q, 3 * B, LANES), F32),
    face1=((4, Q, FB, LANES), F32),
    table=((2 * TABLE, 1024), BF16),
)
CHANGE = dict(
    across=((4, TABLE, LANES), F32),
    zh=((KZ, Q * 256), BF16),
    zl=((KZ, Q * 256), BF16),
)
PREDICT = dict(
    dofs=((Q, B, 256), F32),
    cur=((Q, B, 256), F32),
    term=((Q, B, 256), F32),
    moved=((Q, 3 * B, 256), F32),
)
REMOTE = dict(
    gfield=FIELD,
    edge=((Q, B, 256), F32),
    rtable=((2 * Q * FB, 512), BF16),
    rzh=((KZ, Q * 256), BF16),
    rzl=((KZ, Q * 256), BF16),
)
EVEN = dict(part0=FIELD, base=FIELD, curb=FIELD, curo=((Q, B, 256), F32), **KEPT)
GHOST_MASKS = dict(rhot2=((512, LANES), BF16), rm2=((6, FB, LANES), BF16), ru2=((3, 8, LANES), F32))
STAT = ((STATIC, 8, LANES), F32)
LOADED = ("star", "fluxl", "fluxn", "nbr", "kind", "cluster")
SMALL = ("time", "volume", "project", "rotate", "lift")


def masks(lg):
    shapes = dict(
        hot=((1024, 512), BF16), tm=((6, FB, LANES), BF16), um=((3, 8, LANES), F32),
        fpl=((Q * Q, 8, LANES), F32), fpn=((Q * Q, 8, LANES), F32),
    )
    return {key + str(lg): value for key, value in shapes.items()}


def messages(blocks):
    return {key: ((blocks // 4, 8, LANES), F32) for key in SENT}


def call(kernel, name, ins, outs, scratch, inputs, columns, hbm=False, flops=0, outside=False):
    def body(*refs):
        n, m = len(ins), len(outs)
        r = Bag(zip(ins, refs[:n]))
        o = Bag(zip(outs, refs[n : n + m]))
        s = Bag(zip(scratch, refs[n + m : n + m + len(scratch)]))
        if hbm:
            sems = refs[-1]
            copies = {}
            for k, key in enumerate((*SMALL, "nbr", "kind", "cluster", "dofs", "star", "fluxn", "fluxl")):
                to = o[key] if key in LOADED else s[key + "_in"]
                copies[key] = pltpu.make_async_copy(r[key], to, sems.at[k])
                copies[key].start()
            r = Bag({key: o[key] if key in LOADED else s[key + "_in"] for key in ins})
            kernel(r, o, s, lambda *keys: [copies[key].wait() for key in keys], columns)
        else:
            r.even = place_of(r.nbr, columns)
            kernel(r, o, s)

    shapes = [pltpu.VMEM(*value) if isinstance(value, tuple) else value for value in scratch.values()]
    if hbm:
        shapes.append(pltpu.SemaphoreType.DMA((len(ins),)))
    space = pltpu.HBM if hbm else pltpu.VMEM
    got = pl.pallas_call(
        body,
        out_shape=[jax.ShapeDtypeStruct(*outs[key]) for key in outs],
        in_specs=[pl.BlockSpec(memory_space=space)] * len(ins),
        out_specs=[pl.BlockSpec(memory_space=pltpu.HBM if outside else pltpu.VMEM)] * len(outs),
        scratch_shapes=shapes,
        compiler_params=pltpu.CompilerParams(vmem_limit_bytes=24 << 20),
        cost_estimate=pl.CostEstimate(flops=flops, bytes_accessed=1 << 20, transcendentals=0),
        name=name,
    )(*(pltpu.with_memory_space_constraint(inputs[key], space) if hbm else inputs[key] for key in ins))
    return dict(zip(outs, got))


def fine_of(cluster_ref):
    return (cluster_ref[...] == 0).astype(F32)


def first_kernel(r, o, s, wait, columns):
    wait("time")
    prepare_predictor(r.time, o.wt, s.ptmp)
    wait("volume", "project", "rotate", "lift")
    prepare(r.volume, r.project, r.rotate, r.lift, o.wb, o.wl, s.ptmp, s.pturn, s.pbig)
    wait("nbr", "kind", "cluster")
    build_onehot(r.nbr, r.kind, o, [0])
    wait("dofs")
    for p in range(Q):
        s.dofs[p, 0:20, 0:256] = r.dofs[p]
        s.dofs[p, 20:B, 0:256] = jnp.zeros((B - 20, 256), F32)
    wait("star", "fluxn", "fluxl")
    keep_rows(r.fluxl, 0, o.fpl0)
    keep_rows(r.fluxn, 0, o.fpn0)
    describe(r.nbr, r.kind, r.cluster, r.star, r.fluxn, o.stat)
    r = Bag(r, wt=o.wt, wb=o.wb, wl=o.wl, even=place_of(r.nbr, columns))
    even_half(s | o, r, fine_of(r.cluster), s.dofs, o, o.stat)


def first_rest(r, o, s):
    build_onehot(r.nbr, r.kind, o, [1])
    keep_rows(r.fluxl, 1, o.fpl1)
    keep_rows(r.fluxn, 1, o.fpn1)
    build_remote(r.stat, o.rhot, o.rm, o.ru)
    rest_half(r | o | s, r, o)


def middle_kernel(r, o, s):
    def keep(n, value):
        o.ghost[n] = value

    unpack([r[key] for key in GOT], 54, 54 + STATIC, keep, r.even)
    build_remote(o.ghost, o.rhot2, o.rm2, o.ru2)
    fine = fine_of(r.cluster)
    s = r | s | o
    odd_half(s, r, fine, o.ghost, [s.next.at[:, :, group(lg)] for lg in range(2)])
    even_half(s, r, fine, s.next, o, None)


def second_rest(r, o, s):
    rest_half(r | o | s, r, o)


def last_kernel(r, o, s):
    copies = [pltpu.make_async_copy(s.result.at[p], o.out.at[p], s.sems.at[p]) for p in range(Q)]

    def finish(p, lg, value):
        s.result[p, :, group(lg)] = value[0:20]
        if lg == 1:
            copies[p].start()

    s = r | s
    odd_half(s, r, fine_of(r.cluster), r.ghost, [s.next.at[:, :, group(lg)] for lg in range(2)], finish)
    for copy in copies:
        copy.wait()


def trade(got):
    out = {}
    for m, (axis, start) in enumerate((("px", 0), ("px", 1), ("py", 1), ("py", 0))):
        count = lax.axis_size(axis)
        pairs = []
        for low in range(start, count - 1, 2):
            pairs += [(low, low + 1), (low + 1, low)]
        out[GOT[m]] = lax.ppermute(got[SENT[m]], axis, pairs)
    return out


def per_device(dofs, star, flux_local, flux_neigh, time_stiff, volume_stiff, face_project, face_rotate, face_lift, cluster, neighbors, face_kind):
    columns = lax.axis_size("py")
    inputs = dict(
        dofs=dofs, star=star.transpose(1, 2, 0, 3), fluxl=flux_local.transpose(1, 2, 0, 3),
        fluxn=flux_neigh.transpose(1, 2, 0, 3), time=time_stiff, volume=volume_stiff,
        project=face_project.transpose(1, 0, 2), rotate=face_rotate.transpose(1, 0, 2), lift=face_lift.transpose(2, 0, 1),
        cluster=cluster.reshape(1, 256), nbr=neighbors, kind=face_kind,
    )
    first = {
        **{key: (inputs[key].shape, inputs[key].dtype) for key in LOADED},
        "wt": ((80, 80), BF16),
        "wb": ((144, 80), BF16),
        "wl": ((64, KZ), BF16),
        "stat": STAT,
        **masks(0),
        **EVEN,
        **messages(96),
    }
    scratch = {
        **PREDICT, **SPREAD, **CHANGE, "ptmp": ((144, LANES), F32), "pturn": ((LANES, LANES), F32), "pbig": ((256, LANES), F32),
        **{key + "_in": (inputs[key].shape, inputs[key].dtype) for key in (*SMALL, "dofs")},
    }
    alone = dict(**CHANGE, term1=FIELD, pmoved1=((Q, 3 * B, LANES), F32))
    weights = ["star", "fluxl", "fluxn", "wt", "wb", "wl", "nbr"]
    rest = {"part1": FIELD, "ahead": FIELD, "rtable2": ((2 * Q * FB, 512), BF16)}
    state = ["part0", "part1", "ahead", "rtable2", "curo", *GOT]
    odd = weights + ["cluster", "stat", *masks(0), *masks(1), "rhot", "rm", "ru"] + state
    inputs |= call(first_kernel, "first", list(inputs), first, scratch, inputs, columns, hbm=True)
    inputs |= trade(inputs)
    inputs |= call(
        first_rest, "first_rest", weights + ["kind", "stat", "base", "curb", *KEPT],
        {**rest, **masks(1), "rhot": ((512, LANES), BF16), "rm": ((6, FB, LANES), BF16), "ru": ((3, 8, LANES), F32)},
        alone, inputs, columns, flops=10**9,
    )
    both = {**PREDICT, **SPREAD, **CHANGE, **REMOTE, "next": ((Q, B, 256), F32)}
    inputs |= call(
        middle_kernel, "middle", odd, {"ghost": STAT, **GHOST_MASKS, **EVEN, **messages(56)}, both, inputs, columns,
    )
    inputs |= trade(inputs)
    inputs |= call(
        second_rest, "second_rest", weights + ["base", "curb", *masks(1), *KEPT], rest, alone, inputs, columns,
        flops=10**9,
    )
    got = call(
        last_kernel, "last", odd + ["ghost", *GHOST_MASKS], {"out": ((Q, 20, 256), F32)}, {**both, **KEPT, "result": ((Q, 20, 256), F32), "sems": pltpu.SemaphoreType.DMA((Q,))},
        inputs, columns, outside=True,
    )
    return got["out"]


def solution(mesh):
    cells = ("px", "py")
    placed = (
        P(None, None, cells),
        P(None, None, None, cells),
        P(None, None, None, cells),
        P(None, None, None, cells),
        P(),
        P(),
        P(),
        P(),
        P(),
        P(cells),
        P(None, cells),
        P(None, cells),
    )
    return jax.shard_map(
        per_device,
        mesh=mesh,
        in_specs=placed,
        out_specs=P(None, None, cells),
        check_vma=False,
    )
```
